32 devices in a mesh: wide: 16 (over z, y, x), narrow: 2 (over core).
Axes of the slice: x: 2, y: 2, z: 4, core: 2. Of those that a mesh axis runs over, the one named last changes fastest.
Arguments:
- inputs: bfloat16 [64, 768, 512], P(('wide', 'narrow')), may hold values from -6 to 6
- memory: bfloat16 [64, 96, 512], P(('wide', 'narrow')), may hold values from -6 to 6
- tau_scale: float32 [64], P(('wide', 'narrow')), may hold values from 1 to 3
- delta_shift: float32 [64, 96], P(('wide', 'narrow')), may hold values from -4 to 4
- horizon: int32 [64], P(('wide', 'narrow')), may hold values from 96 to 720, as said below
- memory_mask: int32 [64, 96], P(('wide', 'narrow')), may hold values from 0 to 1, as said below
- cotangent: bfloat16 [64, 768, 512], P(('wide', 'narrow')), may hold values from -6 to 6
- self_weights: bfloat16 [1048576], P(('wide', 'narrow'))
- cross_weights: bfloat16 [1048576], P(('wide', 'narrow'))
- feed_weights: bfloat16 [2097152], P(('wide', 'narrow'))
- small_params: bfloat16 [8704], P(('wide', 'narrow'))
Outputs:
- output: bfloat16 [64, 768, 512], P(('wide', 'narrow'))
- grad_inputs: float32 [64, 768, 512], P(('wide', 'narrow'))
- grad_memory: float32 [64, 96, 512], P(('wide', 'narrow'))
- grad_tau: float32 [64], P(('wide', 'narrow'))
- grad_delta: float32 [64, 96], P(('wide', 'narrow'))
- grad_self: float32 [1048576], P(('wide', 'narrow'))
- grad_cross: float32 [1048576], P(('wide', 'narrow'))
- grad_feed: float32 [2097152], P(('wide', 'narrow'))
- grad_small: float32 [8704], P(('wide', 'narrow'))
The draws below stay inside these ranges and needn't reach their ends.
Inputs may be any that keep to these rules, and one draw needn't show every extreme that they name: Each item's horizon is 720 times 96, 192, 336 or 720, divided by 720 and rounded down; some item has 720 in every draw. `memory_mask`: the last of the 96 memory steps of every item is 1.
All inputs are finite; a program needn't handle non-finite values.
Results may differ from the reference program's by a relative error of at most 0.04.
Values may be sent and summed in bfloat16 or wider, within the bound.
No kernel may reach another device: no remote copies, remote signals or barrier semaphores. Data moves between devices by JAX's collectives and lax.ppermute only.
A program may use at most 192 MiB of HBM per device.

```python
import math
import jax
import jax.numpy as jnp
from jax import lax

D = 512
H = 8
HD = 64
FF = 2048
LABEL = 48
HMAX = 720
MEM = 96
ROWS = 768
ITEMS = 64


def draw_horizon(key, part):
    key = jax.random.fold_in(key, 11)
    first, second = jax.random.split(key)
    picks = jax.random.randint(first, (ITEMS,), 0, 4)
    options = jnp.array([HMAX * 96 // 720, HMAX * 192 // 720, HMAX * 336 // 720, HMAX], jnp.int32)
    lengths = jnp.sum(jnp.where(picks[:, None] == jnp.arange(4)[None, :], options[None, :], 0), axis=1)
    chosen = jax.random.randint(second, (), 0, ITEMS)
    return jnp.where(jnp.arange(ITEMS) == chosen, HMAX, lengths).astype(jnp.int32)


def draw_memory_mask(key, part):
    key = jax.random.fold_in(key, 12)
    levels = jax.random.randint(key, (ITEMS, MEM), 0, 4)
    observed = jnp.where(levels > 0, 1, 0)
    return jnp.where(jnp.arange(MEM)[None, :] == MEM - 1, 1, observed).astype(jnp.int32)


def square_draw(key, out_factor):
    base = jnp.clip(jax.random.normal(key, (4 * D * D,), jnp.float32), -6.0, 6.0)
    scales = jnp.concatenate([jnp.full((3 * D * D,), D ** (-0.5), jnp.float32), jnp.full((D * D,), out_factor * D ** (-0.5), jnp.float32)])
    return (base * scales).astype(jnp.bfloat16)


def draw_self_weights(key, part):
    key = jax.random.fold_in(key, 13)
    return square_draw(key, 3.0)


def draw_cross_weights(key, part):
    key = jax.random.fold_in(key, 14)
    return square_draw(key, 4.0)


def draw_feed_weights(key, part):
    key = jax.random.fold_in(key, 15)
    base = jnp.clip(jax.random.normal(key, (2 * D * FF,), jnp.float32), -6.0, 6.0)
    scales = jnp.concatenate([jnp.full((D * FF,), D ** (-0.5), jnp.float32), jnp.full((D * FF,), 1.5 * FF ** (-0.5), jnp.float32)])
    return (base * scales).astype(jnp.bfloat16)


def draw_small_params(key, part):
    key = jax.random.fold_in(key, 16)
    first, second = jax.random.split(key)
    total = 13 * D + FF
    offsets = 0.3 * jnp.clip(jax.random.normal(first, (total,), jnp.float32), -5.0, 5.0)
    gains = jax.random.uniform(second, (total,), jnp.float32, 0.6, 1.4)
    zero_d = jnp.zeros((D,), jnp.float32)
    one_d = jnp.ones((D,), jnp.float32)
    marks = jnp.concatenate([zero_d, zero_d, zero_d, one_d, zero_d, zero_d, zero_d, zero_d, one_d, zero_d, jnp.zeros((FF,), jnp.float32), zero_d, one_d, zero_d])
    return jnp.where(marks > 0.5, gains, offsets).astype(jnp.bfloat16)


def block_levels(key, dims, shards, least, top_value):
    def one(position, blocks):
        heights = jax.random.uniform(jax.random.fold_in(jax.random.fold_in(key, 6), position), (blocks,), jnp.float32, least / len(shards), top_value / len(shards))
        return jnp.repeat(jnp.exp(heights), dims[position] // blocks).reshape((-1,) + (1,) * (len(dims) - position - 1))

    factor_of = one(*shards[0])
    for cut in shards[1:]:
        factor_of = factor_of * one(*cut)
    return factor_of


def gaussian(key, shape, scale, reach, shards=(), held_as=jnp.bfloat16):
    values = scale * jax.random.normal(key, shape, jnp.float32)
    if shards:
        values = values * block_levels(key, shape, shards, -0.22, 0.18)
    return jnp.clip(values, -reach, reach).astype(held_as)


def setup_inputs(seed: int = 0) -> dict:
    seeds = jax.random.split(jax.random.key(seed), 12)
    inputs = gaussian(seeds[0], (ITEMS, ROWS, D), 1.0, 6.0, ((0, 32),))
    memory = gaussian(seeds[1], (ITEMS, MEM, D), 1.0, 6.0, ((0, 32),))
    tau_scale = jnp.clip(jnp.exp(math.log(3.0) - 1.0986123 * jax.random.uniform(seeds[2], (ITEMS,), jnp.float32) ** block_levels(seeds[2], (ITEMS,), ((0, 32),), -0.2, 0.2)), 1.0, 3.0)
    delta_shift = gaussian(seeds[3], (ITEMS, MEM), 1.0, 4.0, ((0, 32),), jnp.float32)
    horizon = draw_horizon(jax.random.fold_in(seeds[11], 71), 0)
    memory_mask = draw_memory_mask(jax.random.fold_in(seeds[11], 71), 0)
    cotangent = gaussian(seeds[6], (ITEMS, ROWS, D), 1.0, 6.0, ((0, 32),))
    self_weights = draw_self_weights(jax.random.fold_in(seeds[11], 71), 0)
    cross_weights = draw_cross_weights(jax.random.fold_in(seeds[11], 71), 0)
    feed_weights = draw_feed_weights(jax.random.fold_in(seeds[11], 71), 0)
    small_params = draw_small_params(jax.random.fold_in(seeds[11], 71), 0)
    return dict(inputs=inputs, memory=memory, tau_scale=tau_scale, delta_shift=delta_shift, horizon=horizon, memory_mask=memory_mask, cotangent=cotangent, self_weights=self_weights, cross_weights=cross_weights, feed_weights=feed_weights, small_params=small_params)


@jax.custom_vjp
def low(v):
    return lax.optimization_barrier(v.astype(jnp.bfloat16)).astype(jnp.float32)

@jax.custom_vjp
def low_back(v):
    return v

def low_keep(v):
    return (low(v), None)

def low_pass(kept, grad):
    return (grad,)

def back_keep(v):
    return (v, None)

def back_low(kept, grad):
    return (low(grad),)
low.defvjp(low_keep, low_pass)
low_back.defvjp(back_keep, back_low)
highest = lax.Precision.HIGHEST
epsilon = 1e-05

def lower_both(value):
    return low(low_back(value))

def product(left, right):
    return jnp.dot(left, right, precision=highest)

def split_small(vector):
    widths = [D] * 10 + [FF] + [D] * 3
    pieces = []
    start = 0
    for width in widths:
        pieces.append(vector[start:start + width])
        start = start + width
    return pieces

def square_blocks(flat):
    blocks = flat.reshape(4, D, D)
    return (blocks[0], blocks[1], blocks[2], blocks[3])

def layer_norm(summed, gain, offset):
    centred = summed - lax.optimization_barrier(jnp.mean(summed, axis=-1, keepdims=True))
    inverse = lax.rsqrt(lax.optimization_barrier(jnp.mean(centred * centred, axis=-1, keepdims=True)) + epsilon)
    return centred * inverse * gain + offset

def attend(query, keys, values, factor, shift, allowed):
    rows = query.shape[0]
    query_heads = query.reshape(rows, H, HD)
    key_heads = keys.reshape(keys.shape[0], H, HD)
    value_heads = values.reshape(values.shape[0], H, HD)
    raw_scores = jnp.einsum('qhd,khd->hqk', query_heads, key_heads, precision=highest)
    scores = low_back(jnp.where(allowed[None], raw_scores * factor + shift[None, None, :], -1e+30))
    weights = low(jax.nn.softmax(scores, axis=-1))
    attended_values = jnp.einsum('hqk,khd->qhd', weights, value_heads, precision=highest)
    return attended_values.reshape(rows, H * HD)

def layer(params, rows_in, memory_rows, scale_item, shift, length, mask_row):
    self_flat, cross_flat, feed_flat, small = params
    bias_query_one, bias_value_one, bias_out_one, gain_one, offset_one, bias_query_two, bias_value_two, bias_out_two, gain_two, offset_two, bias_up, bias_down, gain_three, offset_three = split_small(small)
    w_query_one, w_key_one, w_value_one, w_out_one = square_blocks(self_flat)
    w_query_two, w_key_two, w_value_two, w_out_two = square_blocks(cross_flat)
    w_up = feed_flat[:D * FF].reshape(D, FF)
    w_down = feed_flat[D * FF:].reshape(FF, D)
    rows = rows_in.shape[0]
    places = jnp.arange(rows)
    causal = places[:, None] >= places[None, :]
    factor = scale_item / math.sqrt(HD)
    query_one = lower_both(product(rows_in, w_query_one) + bias_query_one)
    key_one = lower_both(product(rows_in, w_key_one))
    value_one = lower_both(product(rows_in, w_value_one) + bias_value_one)
    mixed_one = lower_both(attend(query_one, key_one, value_one, factor, jnp.zeros_like(rows_in[:, 0]), causal))
    branch_one = low_back(product(mixed_one, w_out_one) + bias_out_one)
    normed_one = layer_norm(rows_in + branch_one, gain_one, offset_one)
    query_two = lower_both(product(low(normed_one), w_query_two) + bias_query_two)
    key_two = lower_both(product(memory_rows, w_key_two))
    value_two = lower_both(product(memory_rows, w_value_two) + bias_value_two)
    allowed = jnp.broadcast_to(mask_row[None, :] == 1, (rows, MEM))
    mixed_two = lower_both(attend(query_two, key_two, value_two, factor, shift, allowed))
    branch_two = low_back(product(mixed_two, w_out_two) + bias_out_two)
    normed_two = layer_norm(normed_one + branch_two, gain_two, offset_two)
    hidden = low_back(product(low(normed_two), w_up) + bias_up)
    activated = low(jax.nn.gelu(hidden, approximate=False))
    branch_three = low_back(product(activated, w_down) + bias_down)
    normed_three = layer_norm(normed_two + branch_three, gain_three, offset_three)
    valid = places < LABEL + length
    return jnp.where(valid[:, None], normed_three, 0.0)

def reference(inputs, memory, tau_scale, delta_shift, horizon, memory_mask, cotangent, self_weights, cross_weights, feed_weights, small_params):
    params = (self_weights.astype(jnp.float32), cross_weights.astype(jnp.float32), feed_weights.astype(jnp.float32), small_params.astype(jnp.float32))
    total = inputs.shape[0]
    group = math.gcd(total, 4)
    count = total // group

    def regroup(array):
        return array.reshape((count, group) + array.shape[1:])
    batches = tuple((regroup(array) for array in (inputs, memory, tau_scale, delta_shift, horizon, memory_mask, cotangent)))

    def step(carry, batch):
        rows_in, memory_rows, scale_item, shift, length, mask_row, cot_rows = batch

        def forward(weights, rows_value, memory_value, scale_value, shift_value):
            return jax.vmap(layer, in_axes=(None, 0, 0, 0, 0, 0, 0))(weights, rows_value, memory_value, scale_value, shift_value, length, mask_row)
        result, pull = jax.vjp(forward, params, rows_in.astype(jnp.float32), memory_rows.astype(jnp.float32), scale_item, shift)
        grads = pull(cot_rows.astype(jnp.float32))
        carry = tuple((left + right for left, right in zip(carry, grads[0])))
        return (carry, (result.astype(jnp.bfloat16), grads[1], grads[2], grads[3], grads[4]))
    start_sums = tuple((jnp.zeros_like(param) for param in params))
    sums, stacked = lax.scan(step, start_sums, batches)

    def flatten(array):
        return array.reshape((total,) + array.shape[2:])
    return (flatten(stacked[0]), flatten(stacked[1]), flatten(stacked[2]), flatten(stacked[3]), flatten(stacked[4]), sums[0], sums[1], sums[2], sums[3])
```

```python
import math

import jax
import jax.numpy as jnp
from jax import lax
from jax.experimental import pallas as pl
from jax.experimental.pallas import tpu as pltpu
from jax.sharding import PartitionSpec as P

D = 512
H = 8
HD = 64
FF = 2048
LABEL = 48
EPS = 1e-05
LOG2E = math.log2(math.e)
LN2 = math.log(2.0)
MASKED = -1e30 * LOG2E
QB = 256
GROUPS = (2, 2)
FEED_ROWS = 512
FEED_SUBS = 2
ROWS = 768
W = ("wide", "narrow")
SMALL = 16
bf16 = jnp.bfloat16
f32 = jnp.float32


def nn(a, b):
    return lax.dot_general(a, b, (((1,), (0,)), ((), ())), preferred_element_type=f32)


def nt(a, b):
    return lax.dot_general(a, b, (((1,), (1,)), ((), ())), preferred_element_type=f32)


def tn(a, b):
    return lax.dot_general(a, b, (((0,), (0,)), ((), ())), preferred_element_type=f32)


def upright(row):
    return jnp.broadcast_to(row, (128, row.shape[1])).T[:, :1]


def any_spec():
    return pl.BlockSpec(memory_space=pl.ANY)


def whole(shape):
    return pl.BlockSpec(shape, lambda *_: (0,) * len(shape))


def smem():
    return pl.BlockSpec(memory_space=pltpu.SMEM)


def params(mib):
    return pltpu.CompilerParams(
        vmem_limit_bytes=mib * 1024 * 1024, dimension_semantics=("arbitrary",)
    )


def cost(flops, nbytes, trans=0):
    return pl.CostEstimate(flops=int(flops), bytes_accessed=int(nbytes), transcendentals=int(trans))


def in_hbm(v):
    return pltpu.with_memory_space_constraint(v, pltpu.HBM)


def sds(shape, dtype):
    return jax.ShapeDtypeStruct(shape, dtype)


def place_square(s):
    return [(0, 64, 64 * s)]


def my_index():
    return lax.axis_index("wide") * 2 + lax.axis_index("narrow")


def aligned(row):
    return row if isinstance(row, int) else pl.multiple_of(row, 32)


def fetch(refs, plan, unit, place, dst, sem, extra=None):
    if plan is None:
        pltpu.make_async_copy(refs[0], dst, sem).start()
    else:
        for ref, held in zip(refs, plan):
            for i, (piece, other) in enumerate(held):
                for src, size, row in place(piece_owners(piece, other)):
                    pltpu.make_async_copy(
                        ref.at[pl.ds(i * unit + src, size)],
                        dst.at[pl.ds(aligned(row), size)],
                        sem,
                    ).start()
        if extra is not None:
            for k, (ref, held) in enumerate(zip(refs, plan)):
                pltpu.make_async_copy(
                    ref.at[pl.ds(len(held) * unit, SMALL)], extra.at[pl.ds(k * SMALL, SMALL)], sem
                ).start()
            pltpu.make_async_copy(extra, extra, sem).wait()
    pltpu.make_async_copy(dst, dst, sem).wait()


def deliver(src, refs, plan, unit, place, sem, extra=None):
    if plan is None:
        pltpu.make_async_copy(src, refs[0], sem).start()
    else:
        for ref, held in zip(refs, plan):
            for i, (piece, other) in enumerate(held):
                for dst, size, row in place(piece_owners(piece, other)):
                    pltpu.make_async_copy(
                        src.at[pl.ds(aligned(row), size)],
                        ref.at[pl.ds(i * unit + dst, size)],
                        sem,
                    ).start()
        if extra is not None:
            for ref, held in zip(refs, plan):
                pltpu.make_async_copy(extra, ref.at[pl.ds(len(held) * unit, SMALL)], sem).start()
            for _ in refs:
                pltpu.make_async_copy(extra, extra, sem).wait()
    pltpu.make_async_copy(src, src, sem).wait()


def fetch_blocks(refs, plan, dst, sem):
    if plan is None:
        pltpu.make_async_copy(refs[0], dst, sem).start()
    else:
        for ref, held in zip(refs, plan):
            for i, (piece, other) in enumerate(held):
                pltpu.make_async_copy(ref.at[i], dst.at[piece_owners(piece, other)], sem).start()
    pltpu.make_async_copy(dst, dst, sem).wait()


def deliver_blocks(src, refs, plan, sem, first_half):
    half = src.shape[0] // 2
    here = slice(0, half) if first_half else slice(half, 2 * half)
    if plan is None:
        pltpu.make_async_copy(src.at[here], refs[0].at[here], sem).start()
        return
    for ref, held in zip(refs, plan):
        for i, (piece, other) in enumerate(held):
            owner = piece_owners(piece, other)

            @pl.when((owner < half) if first_half else (owner >= half))
            def _():
                pltpu.make_async_copy(src.at[owner], ref.at[i], sem).start()


def swap(v):
    return lax.ppermute(v, "narrow", [(0, 1), (1, 0)])


def special():
    return lax.axis_size("wide") == 16 and lax.axis_size("narrow") == 2


CORE_MASKS = ((1, 2), (2, 1))
COLUMN = (0, 4, 8, 12)


def core_hop(v, stage):
    n = lax.axis_size("wide")
    return lax.ppermute(
        v, W, [(2 * i + c, 2 * (i ^ CORE_MASKS[c][stage]) + c) for i in range(n) for c in range(2)]
    )


def column_hop(v, mask):
    n = lax.axis_size("wide")
    return lax.ppermute(v, "wide", [(i, i ^ mask) for i in range(n)])


def masks_of(core):
    return [jnp.where(core == 0, a, b) for a, b in zip(*CORE_MASKS)]


def wide_mask(q, masks):
    total = COLUMN[q % 4]
    for bit, mask in zip((8, 4), masks):
        if q & bit:
            total = total + mask
    return total


def piece_owners(q, other):
    core = lax.axis_index("narrow")
    wide = lax.axis_index("wide")
    core = 1 - core if other else core
    return (wide ^ wide_mask(q, masks_of(core))) * 2 + core


GATHER_PLAN = tuple(
    tuple((q, other) for q in qs)
    for other in (False, True)
    for qs in ((0, 1, 2, 3, 4, 5, 6, 7), (8, 9, 10, 11, 12, 13, 14, 15))
)
SCATTER_PLAN = tuple(tuple((q, other) for q in range(16)) for other in (False, True))


def after(v, *others):
    return lax.optimization_barrier((v,) + others)[0]


def pad_rows(v):
    return jnp.pad(v, ((0, SMALL - v.shape[0]), (0, 0)))


def join(parts, extra=0):
    if not extra:
        return jnp.concatenate(parts)
    n = parts[0].shape[0] - extra
    return jnp.concatenate([p[:n] for p in parts] + [sum(p[n:] for p in parts[1:]) + parts[0][n:]])


def gather_column(own):
    far = [column_hop(own, mask) for mask in COLUMN[:0:-1]]
    return [own] + far[::-1]


def gather_stage(held, stage, extra=0):
    return join([held, core_hop(held, stage)], extra)


def add(*terms):
    total = terms[0].astype(f32)
    for term in terms[1:]:
        total = total + term.astype(f32)
    return total


def fold(arrays, outputs):
    n = len(arrays)

    def kernel(*refs):
        for out, (dtype, segments) in zip(refs[n:], outputs):
            at = 0
            for height, terms in segments:
                total = add(*[refs[i][first : first + height] for i, first in terms])
                out[at : at + height] = total.astype(dtype)
                at += height

    in_vmem = pl.BlockSpec(memory_space=pltpu.VMEM)
    shapes = [sds((sum(h for h, _ in segments), D), dtype) for dtype, segments in outputs]
    return pl.pallas_call(
        kernel,
        in_specs=[in_vmem] * n,
        out_specs=[in_vmem] * len(outputs),
        out_shape=shapes,
        compiler_params=pltpu.CompilerParams(vmem_limit_bytes=16 * 1024 * 1024),
        cost_estimate=cost(1e6, sum(v.size * 2 for v in arrays)),
        name="fold",
    )(*arrays)


class Scatter:
    def __init__(self, keep, send, unit, extra=0):
        self.unit, self.extra = unit, extra
        self.keep, self.came = keep, swap(send)

    def wait(self, *others):
        self.came = after(self.came, *others)

    def first(self):
        half = 8 * self.unit
        if self.extra:
            (self.sent,) = fold(
                [self.keep, self.came], [(bf16, [(half + self.extra, [(0, half), (1, half)])])]
            )
            self.kept = [self.keep, self.came]
        else:
            self.sent = add(self.keep[half:], self.came[half:]).astype(bf16)
            self.kept = [add(self.keep[:half], self.came[:half]).astype(bf16)]
        self.came = core_hop(self.sent, 0)
        return self.sent

    def second(self):
        half, n = 4 * self.unit, len(self.kept)
        sent = [(half, [(i, half) for i in range(n + 1)])]
        if self.extra:
            sent.append((self.extra, [(n, 2 * half), (n + 1, 2 * half)]))
        self.sent, self.kept = fold(
            self.kept + [self.came, self.sent],
            [(bf16, sent), (f32, [(half, [(i, 0) for i in range(n + 1)])])],
        )
        self.came = core_hop(self.sent, 1)
        return self.sent

    def column(self):
        unit = self.unit
        outputs = [(f32, [(unit, [(0, 0), (1, 0)])])]
        for z in range(1, 4):
            outputs.append((bf16, [(unit, [(0, z * unit), (1, z * unit)])]))
            if self.extra:
                outputs[z][1].append((self.extra, [(1, 4 * unit), (2, 4 * unit)]))
        outs = fold([self.kept, self.came, self.sent], outputs)
        self.kept, self.sent = outs[0], outs[1]
        self.came = [None] + [column_hop(v, COLUMN[z]) for z, v in zip((3, 2, 1), outs[:0:-1])]
        return outs[3]

    def wait_column(self, *others):
        self.came[1:] = lax.optimization_barrier(tuple(self.came[1:]) + others)[:3]

    def total(self):
        outputs = [(f32, [(self.unit, [(i, 0) for i in range(4)])])]
        if self.extra:
            outputs.append((f32, [(self.extra, [(i, self.unit) for i in range(1, 5)])]))
        return fold([self.kept] + self.came[1:] + [self.sent], outputs)


def norm_forward(s):
    centred = s - jnp.mean(s, axis=-1, keepdims=True)
    inverse = lax.rsqrt(jnp.mean(centred * centred, axis=-1, keepdims=True) + EPS)
    return centred * inverse, inverse


def norm_backward(grad, normal, inverse, gain):
    scaled = grad * gain
    grad_in = inverse * (
        scaled
        - jnp.mean(scaled, axis=-1, keepdims=True)
        - normal * jnp.mean(scaled * normal, axis=-1, keepdims=True)
    )
    return (
        grad_in,
        jnp.sum(grad * normal, axis=0, keepdims=True),
        jnp.sum(grad, axis=0, keepdims=True),
    )


def gelu_parts(u):
    cumulative = 0.5 + 0.5 * lax.erf(u * math.sqrt(0.5))
    density = jnp.exp2(u * u * (-0.5 * LOG2E)) * (1.0 / math.sqrt(2.0 * math.pi))
    return u * cumulative, cumulative + u * density


def pipeline(units, *stages):
    held = {}
    for turn in range(len(units) + max(delay for delay, _ in stages)):
        for delay, stage in stages:
            at = turn - delay
            if 0 <= at < len(units):
                held[at] = stage(units[at], held.get(at))


def interleave(streams):
    live = list(streams)
    while live:
        live = [stream for stream in live if next(stream, live) is not live]


def small_rows(w, extra, plan):
    if plan is None:
        return w[4 * D :].astype(f32)
    return add(*[extra[k * SMALL : (k + 1) * SMALL] for k in range(extra.shape[0] // SMALL)])


def project_self(x, pieces, plan, tau):
    total = x.shape[0]
    per_item = total // (tau.shape[0] * ROWS)
    n = len(pieces)
    full = 4 * D + SMALL if plan is None else 4 * D

    def kernel(*refs):
        piece_refs = refs[:n]
        x_ref, tau_ref, q_ref, k_ref, v_ref, wt_ref, wo_ref, w, extra, cols, sem = refs[n:]
        step = pl.program_id(0)

        @pl.when(step == 0)
        def _():
            fetch(piece_refs, plan, 64, place_square, w, sem, extra)
            small = small_rows(w, extra, plan)
            cols[0] = upright(small[0:1])
            cols[1] = upright(small[1:2])
            for m in range(3):
                wt_ref[m * D : (m + 1) * D] = w[m * D : (m + 1) * D].T
            wo_ref[...] = w[3 * D : 4 * D]

        factor = tau_ref[lax.div(step, per_item)] * (LOG2E / math.sqrt(HD))
        rows_in = x_ref[...]
        q_ref[...] = ((nt(wt_ref[:D], rows_in) + cols[0]) * factor).astype(bf16)
        k_ref[...] = nt(wt_ref[D : 2 * D], rows_in).astype(bf16)
        v_ref[...] = (nt(wt_ref[2 * D :], rows_in) + cols[1]).astype(bf16)

    feature = pl.BlockSpec((D, ROWS), lambda i: (0, i))
    return pl.pallas_call(
        kernel,
        grid=(total // ROWS,),
        in_specs=[any_spec()] * n
        + [pl.BlockSpec((ROWS, D), lambda i: (i, 0)), smem()],
        out_specs=[feature] * 3 + [whole((3 * D, D)), whole((D, D))],
        out_shape=[sds((D, total), bf16)] * 3
        + [sds((3 * D, D), bf16), sds((D, D), bf16)],
        scratch_shapes=[
            pltpu.VMEM((full, D), bf16),
            pltpu.VMEM((n * SMALL, D), bf16),
            pltpu.VMEM((2, D, 1), f32),
            pltpu.SemaphoreType.DMA,
        ],
        compiler_params=params(56),
        cost_estimate=cost(6 * total * D * D, 12e6),
        name="project_self",
    )(*pieces, x, tau)


def block_start(j):
    return j * (j + 1) // 2


def attend_self(first, pairs, q, k, v, items, rows):
    blocks = rows // QB
    count = block_start(blocks)
    heads = 2 * pairs

    def kernel(q_ref, k_ref, v_ref, e_ref, o_ref, l_ref, vaug):
        key_place = lax.broadcasted_iota(jnp.int32, (QB, QB), 0)
        query_place = lax.broadcasted_iota(jnp.int32, (QB, QB), 1)
        allowed = key_place <= query_place
        for h in range(heads):
            vaug[h, :HD] = v_ref[h * HD : (h + 1) * HD]
            vaug[h, HD:] = jnp.ones((16, rows), bf16)

        def score(unit, _):
            h, j = unit
            span = slice(h * HD, (h + 1) * HD)
            return tn(k_ref[span, : (j + 1) * QB], q_ref[span, j * QB : (j + 1) * QB])

        def weigh(unit, scores):
            h, j = unit
            diagonal = jnp.where(allowed, scores[j * QB :], MASKED)
            top = jnp.max(diagonal, axis=0, keepdims=True)
            if j:
                top = jnp.maximum(top, jnp.max(scores[: j * QB], axis=0, keepdims=True))
            weights = []
            for b in range(j + 1):
                part = diagonal if b == j else scores[b * QB : (b + 1) * QB]
                weight = jnp.exp2(part - top).astype(bf16)
                e_ref[0, h, block_start(j) + b] = weight
                weights.append(weight)
            return jnp.concatenate(weights, axis=0) if j else weights[0]

        def mix(unit, weights):
            h, j = unit
            here = slice(j * QB, (j + 1) * QB)
            mixed = nn(vaug[h, :, : (j + 1) * QB], weights)
            inverse = 1.0 / mixed[HD : HD + 1]
            o_ref[h * HD : (h + 1) * HD, here] = (mixed[:HD] * inverse).astype(bf16)
            l_ref[h // 2, h % 2 : h % 2 + 1, here] = inverse

        units = [(h, j) for j in range(blocks) for h in range(heads)]
        pipeline(units, (0, score), (2, weigh), (3, mix))

    total = items * rows
    height = heads * HD
    feature = pl.BlockSpec((height, rows), lambda i: (first // pairs, i))
    return pl.pallas_call(
        kernel,
        grid=(items,),
        in_specs=[feature] * 3,
        out_specs=[
            pl.BlockSpec((1, heads, count, QB, QB), lambda i: (i, 0, 0, 0, 0)),
            pl.BlockSpec((height, rows), lambda i: (0, i)),
            pl.BlockSpec((pairs, 8, rows), lambda i: (0, 0, i)),
        ],
        out_shape=[
            pltpu.HBM((items, heads, count, QB, QB), bf16),
            sds((height, total), bf16),
            sds((pairs, 8, total), f32),
        ],
        scratch_shapes=[pltpu.VMEM((heads, HD + 16, rows), bf16)],
        compiler_params=params(56),
        cost_estimate=cost(4 * 4 * pairs * items * 2 * rows * rows * HD, 8e6 * pairs / 2),
        name="attend_self",
    )(q, k, v)


def cross_forward(x, mixed, wo1, pieces, plan, tau, memory, shift, mask):
    items, slots = memory.shape[0], memory.shape[1]
    total = x.shape[0]
    rows = total // items
    blocks = rows // ROWS
    n = len(pieces)
    n_mixed = len(mixed)

    def kernel(*refs):
        piece_refs = refs[:n]
        mixed_refs = refs[n : n + n_mixed]
        x_ref, wo1_ref, tau_ref, mem_ref, shift_ref, mask_ref = refs[n + n_mixed : n + n_mixed + 6]
        (
            n1_ref, i1_ref, n2_ref, i2_ref, q_ref, k_ref, v_ref, e_ref, l_ref, o_ref,
            wt_ref, wo2_ref, small_ref, w, extra, cols, vaug, sem,
        ) = refs[n + n_mixed + 6 :]
        step = pl.program_id(0)
        item = lax.div(step, blocks)

        @pl.when(step == 0)
        def _():
            fetch(piece_refs, plan, 64, place_square, w, sem, extra)
            small_ref[2:17] = small_rows(w, extra, plan)[:15]
            cols[0] = upright(small_ref[5:6])
            cols[1] = upright(small_ref[6:7])
            for m in range(3):
                wt_ref[m * D : (m + 1) * D] = w[m * D : (m + 1) * D].T
            wo2_ref[...] = w[3 * D : 4 * D]

        mixed_one = jnp.concatenate([ref[...] for ref in mixed_refs], axis=0)
        summed = x_ref[...].astype(f32) + tn(mixed_one, wo1_ref[...]) + small_ref[2:3]
        normal, inverse = norm_forward(summed)
        n1_ref[...] = normal.astype(bf16)
        i1_ref[...] = inverse
        y1 = normal * small_ref[3:4] + small_ref[4:5]
        y1_low = y1.astype(bf16)
        factor = tau_ref[item] * (LOG2E / math.sqrt(HD))
        q_ref[...] = ((nt(wt_ref[:D], y1_low) + cols[0]) * factor).astype(bf16)

        @pl.when(step == item * blocks)
        def _():
            mem = mem_ref[0]
            k_ref[0] = nt(wt_ref[D : 2 * D], mem).astype(bf16)
            v_ref[0] = (nt(wt_ref[2 * D :], mem) + cols[1]).astype(bf16)
            for h in range(H):
                vaug[h, :HD] = v_ref[0, h * HD : (h + 1) * HD]
                vaug[h, HD:] = jnp.ones((16, slots), bf16)

        bias = upright(shift_ref[pl.ds(item, 1)] * LOG2E)
        allowed = upright(mask_ref[pl.ds(item, 1)].astype(f32)) == 1.0

        def score(h, _):
            span = slice(h * HD, (h + 1) * HD)
            return tn(k_ref[0, span], q_ref[span])

        def weigh(h, scores):
            scores = jnp.where(allowed, scores + bias, MASKED)
            top = jnp.max(scores, axis=0, keepdims=True)
            weight = jnp.exp2(scores - top).astype(bf16)
            e_ref[0, h] = weight
            return weight

        def mix(h, weight):
            got = nn(vaug[h], weight)
            inv = 1.0 / got[HD : HD + 1]
            l_ref[0, h : h + 1] = inv
            o_ref[h * HD : (h + 1) * HD] = (got[:HD] * inv).astype(bf16)

        pipeline(range(H), (0, score), (2, weigh), (3, mix))
        summed = y1 + tn(o_ref[...], wo2_ref[...]) + small_ref[7:8]
        normal, inverse = norm_forward(summed)
        n2_ref[...] = normal.astype(bf16)
        i2_ref[...] = inverse

    row_block = pl.BlockSpec((ROWS, D), lambda i: (i, 0))
    thin = pl.BlockSpec((ROWS, 1), lambda i: (i, 0))
    feature = pl.BlockSpec((D, ROWS), lambda i: (0, i))
    item3 = lambda a, b: pl.BlockSpec((1, a, b), lambda i: (i // blocks, 0, 0))
    return pl.pallas_call(
        kernel,
        grid=(total // ROWS,),
        in_specs=[any_spec()] * n
        + [pl.BlockSpec((m.shape[0], ROWS), lambda i: (0, i)) for m in mixed]
        + [row_block, whole((D, D)), smem(), item3(slots, D),
           whole((items, slots)), whole((items, slots))],
        out_specs=[
            row_block, thin, row_block, thin, feature, item3(D, slots), item3(D, slots),
            pl.BlockSpec((1, H, slots, ROWS), lambda i: (i // blocks, 0, 0, i % blocks)),
            pl.BlockSpec((1, H, ROWS), lambda i: (i // blocks, 0, i % blocks)), feature,
            whole((3 * D, D)), whole((D, D)), whole((24, D)),
        ],
        out_shape=[
            sds((total, D), bf16), sds((total, 1), f32),
            sds((total, D), bf16), sds((total, 1), f32), sds((D, total), bf16),
            sds((items, D, slots), bf16), sds((items, D, slots), bf16),
            sds((items, H, slots, rows), bf16), sds((items, H, rows), f32), sds((D, total), bf16),
            sds((3 * D, D), bf16), sds((D, D), bf16), sds((24, D), f32),
        ],
        scratch_shapes=[
            pltpu.VMEM((4 * D + (SMALL if plan is None else 0), D), bf16),
            pltpu.VMEM((n * SMALL, D), bf16),
            pltpu.VMEM((2, D, 1), f32),
            pltpu.VMEM((H, HD + 16, slots), bf16),
            pltpu.SemaphoreType.DMA,
        ],
        compiler_params=params(56),
        cost_estimate=cost(9 * total * D * D, 20e6),
        name="cross_forward",
    )(*pieces, *mixed, x, wo1, tau, memory, shift, mask)


def piece_shapes(plan, rows, full_rows, extra=0):
    if plan is None:
        return [sds((full_rows + extra, D), bf16)]
    return [sds((len(held) * rows + extra, D), bf16) for held in plan]


def feed(n2, i2, pieces, plan, out_plan, small, horizon, cotangent, rows):
    total = n2.shape[0]
    block = FEED_ROWS
    subs = FEED_SUBS
    size = block // subs
    steps = total // block
    per_item = rows // size
    out_pieces = [sds((32 if out_plan is None else len(h), 4, 32, D), bf16) for h in out_plan or [()]]
    m = len(out_pieces)
    n = len(pieces)

    def kernel(*refs):
        piece_refs = refs[:n]
        n2_ref, i2_ref, small_ref, horizon_ref, cot_ref = refs[n : n + 5]
        out_ref, ds2_ref, sg_ref = refs[n + 5 : n + 8]
        give_refs = refs[n + 8 : n + 8 + m]
        w_ref, acts, grads, y2s, dzs, slopes, pay, sem = refs[n + 8 + m :]
        step = pl.program_id(0)

        @pl.when(step == 0)
        def _():
            fetch_blocks(piece_refs, plan, w_ref, sem)
            sg_ref[...] = jnp.zeros_like(sg_ref)

        def up(c):
            return w_ref[:16, c].reshape(D, D)

        def down(c):
            return w_ref[16 + 4 * c : 20 + 4 * c].reshape(D, D)

        def one(sub):
            local = slice(sub * size, (sub + 1) * size)
            here = pl.ds(pl.multiple_of(step * block + sub * size, size), size)
            n2 = n2_ref[local].astype(f32)
            y2 = n2 * small_ref[8:9] + small_ref[9:10]
            y2_low = y2.astype(bf16)
            y2s[here] = y2_low
            ahead = nn(y2_low, up(0))
            yield
            summed = y2 + small_ref[14:15]
            for c in range(4):
                cols = slice(c * D, (c + 1) * D)
                hidden = ahead + small_ref[10 + c : 11 + c]
                if c < 3:
                    ahead = nn(y2_low, up(c + 1))
                act, slope = gelu_parts(hidden)
                slopes[sub, c] = slope
                act = act.astype(bf16)
                acts[here, cols] = act
                yield
                summed = summed + nn(act, down(c))
                yield
            normal, inverse = norm_forward(summed)
            position = step * subs + sub
            item = lax.div(position, per_item)
            place = (position - item * per_item) * size
            place = place + lax.broadcasted_iota(jnp.int32, (size, 1), 0)
            valid = place < LABEL + horizon_ref[item]
            gain = small_ref[15:16]
            out_ref[local] = jnp.where(valid, normal * gain + small_ref[16:17], 0.0).astype(bf16)
            yield
            grad = jnp.where(valid, cot_ref[local].astype(f32), 0.0)
            ds3, dg3, dc3 = norm_backward(grad, normal, inverse, gain)
            dz = ds3.astype(bf16)
            dzs[here] = dz
            sg_ref[6:7] += jnp.sum(dz.astype(f32), axis=0, keepdims=True)
            sg_ref[7:8] += dg3
            sg_ref[8:9] += dc3
            yield
            dy2 = ds3
            ahead = nt(dz, down(0))
            yield
            for c in range(4):
                du = ahead * slopes[sub, c]
                if c < 3:
                    ahead = nt(dz, down(c + 1))
                du = du.astype(bf16)
                grads[here, c * D : (c + 1) * D] = du
                sg_ref[2 + c : 3 + c] += jnp.sum(du.astype(f32), axis=0, keepdims=True)
                yield
                dy2 = dy2 + nt(du, up(c))
                yield
            ds2, dg2, dc2 = norm_backward(dy2, n2, i2_ref[local], small_ref[8:9])
            ds2_ref[local] = ds2.astype(bf16)
            sg_ref[0:1] += dg2
            sg_ref[1:2] += dc2
            yield

        interleave([one(sub) for sub in range(subs)])

        @pl.when(step == steps - 1)
        def _():
            pay[16:] = tn(acts[...], dzs[...]).astype(bf16).reshape(16, 4, 32, D)
            deliver_blocks(pay, give_refs, out_plan, sem, False)
            grad = tn(y2s[...], grads[...]).astype(bf16)
            for c in range(4):
                pay[:16, c] = grad[:, c * D : (c + 1) * D].reshape(16, 32, D)
            deliver_blocks(pay, give_refs, out_plan, sem, True)
            pltpu.make_async_copy(pay, pay, sem).wait()

    row_block = pl.BlockSpec((block, D), lambda i: (i, 0))
    outs = pl.pallas_call(
        kernel,
        grid=(steps,),
        in_specs=[any_spec()] * n
        + [
            row_block, pl.BlockSpec((block, 1), lambda i: (i, 0)), whole((24, D)), smem(), row_block,
        ],
        out_specs=[row_block, row_block, whole((16, D))] + [any_spec()] * m,
        out_shape=[sds((total, D), bf16), sds((total, D), bf16), sds((16, D), f32)] + out_pieces,
        scratch_shapes=[
            pltpu.VMEM((32, 4, 32, D), bf16),
            pltpu.VMEM((total, FF), bf16),
            pltpu.VMEM((total, FF), bf16),
            pltpu.VMEM((total, D), bf16),
            pltpu.VMEM((total, D), bf16),
            pltpu.VMEM((subs, 4, size, D), f32),
            pltpu.VMEM((32, 4, 32, D), bf16),
            pltpu.SemaphoreType.DMA,
        ],
        compiler_params=params(56),
        cost_estimate=cost(12 * total * D * FF, 20e6),
        name="feed",
    )(*[v.reshape(-1, 4, 32, D) for v in pieces], n2, i2, small, horizon, cotangent)
    return outs[0], outs[1], outs[2], [v.reshape(-1, D) for v in outs[3:]]


def cross_backward(ds2, q, k, v, e, l, o, wo2, tau, items, rows):
    total = items * rows
    slots = k.shape[2]

    def kernel(
        ds2_ref, q_ref, k_ref, v_ref, e_ref, l_ref, o_ref, wo2_ref, tau_ref,
        dq_ref, dk_ref, dv_ref, tau_out, shift_out, dwo2_ref, sg_ref, acc, do2,
    ):
        item = pl.program_id(0)

        @pl.when(item == 0)
        def _():
            acc[...] = jnp.zeros_like(acc)
            sg_ref[...] = jnp.zeros_like(sg_ref)

        da2 = ds2_ref[...]
        do2[...] = nt(wo2_ref[...], da2)
        factor = tau_ref[item] * (1.0 / math.sqrt(HD))
        sums = [jnp.zeros((slots, rows), f32), jnp.zeros((HD, rows), f32)]

        def spread(h, _):
            span = slice(h * HD, (h + 1) * HD)
            scaled = (do2[span].astype(bf16).astype(f32) * l_ref[0, h : h + 1]).astype(bf16)
            row_term = jnp.sum(scaled.astype(f32) * o_ref[span].astype(f32), axis=0, keepdims=True)
            return scaled, row_term, tn(v_ref[0, span], scaled)

        def weigh(h, given):
            scaled, row_term, slope = given
            ds = (e_ref[0, h].astype(f32) * (slope - row_term)).astype(bf16)
            sums[0] = sums[0] + ds.astype(f32)
            return scaled, ds

        def mix(h, given):
            scaled, ds = given
            span = slice(h * HD, (h + 1) * HD)
            raw = nn(k_ref[0, span], ds)
            sums[1] = sums[1] + raw * q_ref[span].astype(f32)
            dq_ref[span] = (raw * factor).astype(bf16)
            dk_ref[0, span] = (nt(q_ref[span], ds) * LN2).astype(bf16)
            dv_ref[0, span] = nt(scaled, e_ref[0, h]).astype(bf16)

        pipeline(range(H), (0, spread), (2, weigh), (3, mix))
        acc[...] += nn(o_ref[...], da2)
        shift_sum, tau_sum = sums
        shift_out[0] = jnp.broadcast_to(jnp.sum(shift_sum, axis=1, keepdims=True), (slots, 128))
        tau_out[0] = jnp.sum(tau_sum, axis=0, keepdims=True)
        sg_ref[0:1] += nt(jnp.ones((8, rows), bf16), dq_ref[...])[:1]
        sg_ref[1:2] += nt(jnp.ones((8, slots), bf16), dv_ref[0])[:1]
        sg_ref[2:3] += jnp.sum(da2.astype(f32), axis=0, keepdims=True)

        @pl.when(item == items - 1)
        def _():
            dwo2_ref[...] = acc[...].astype(bf16)

    feature = pl.BlockSpec((D, rows), lambda i: (0, i))
    item3 = lambda a, b: pl.BlockSpec((1, a, b), lambda i: (i, 0, 0))
    return pl.pallas_call(
        kernel,
        grid=(items,),
        in_specs=[
            pl.BlockSpec((rows, D), lambda i: (i, 0)), feature, item3(D, slots), item3(D, slots),
            pl.BlockSpec((1, H, slots, rows), lambda i: (i, 0, 0, 0)), item3(H, rows), feature,
            whole((D, D)), smem(),
        ],
        out_specs=[
            feature, item3(D, slots), item3(D, slots), item3(1, rows), item3(slots, 128),
            whole((D, D)), whole((8, D)),
        ],
        out_shape=[
            sds((D, total), bf16), sds((items, D, slots), bf16), sds((items, D, slots), bf16),
            sds((items, 1, rows), f32), sds((items, slots, 128), f32), sds((D, D), bf16),
            sds((8, D), f32),
        ],
        scratch_shapes=[pltpu.VMEM((D, D), f32), pltpu.VMEM((D, rows), f32)],
        compiler_params=params(56),
        cost_estimate=cost(6 * total * D * D, 15e6),
        name="cross_backward",
    )(ds2, q, k, v, e, l, o, wo2, tau)


def between_backward(
    dq, dk, dv, ds2, n1, i1, mixed, memory, wt2, wo1, dwo2, sg_cross, sg_feed, out_plan, small,
    items, rows
):
    total = items * rows
    slots = memory.shape[1]
    n_mixed = len(mixed)
    out_pieces = piece_shapes(out_plan, 64, 4 * D, SMALL)
    m = len(out_pieces)

    def kernel(*refs):
        mixed_refs = refs[:n_mixed]
        (
            dq_ref, dk_ref, dv_ref, ds2_ref, n1_ref, i1_ref, mem_ref, wt_ref, wo1_ref,
            dwo2_ref, cross_ref, feed_ref, small_ref, ds1_ref, do1_ref, gm_ref, dwo1_ref,
        ) = refs[n_mixed : n_mixed + 17]
        give_refs = refs[n_mixed + 17 : n_mixed + 17 + m]
        acc, sg_ref, pay, extra, sem = refs[n_mixed + 17 + m :]
        item = pl.program_id(0)

        @pl.when(item == 0)
        def _():
            acc[...] = jnp.zeros_like(acc)
            sg_ref[...] = jnp.zeros_like(sg_ref)

        dy1 = tn(dq_ref[...], wt_ref[:D]) + ds2_ref[...].astype(f32)
        normal = n1_ref[...].astype(f32)
        acc[0] += nn(dq_ref[...], (normal * small_ref[3:4] + small_ref[4:5]).astype(bf16))
        ds1, dg1, dc1 = norm_backward(dy1, normal, i1_ref[...], small_ref[3:4])
        da1 = ds1.astype(bf16)
        ds1_ref[...] = da1
        sg_ref[1:2] += dg1
        sg_ref[2:3] += dc1
        sg_ref[0:1] += jnp.sum(da1.astype(f32), axis=0, keepdims=True)
        do1_ref[...] = nt(wo1_ref[...], da1).astype(bf16)
        mixed_one = jnp.concatenate([ref[...] for ref in mixed_refs], axis=0)
        acc[3] += nn(mixed_one, da1)
        mem = mem_ref[0]
        acc[1] += nn(dk_ref[0], mem)
        acc[2] += nn(dv_ref[0], mem)
        gm_ref[0] = tn(dk_ref[0], wt_ref[D : 2 * D]) + tn(dv_ref[0], wt_ref[2 * D :])

        @pl.when(item == items - 1)
        def _():
            for i in range(3):
                pay[i * D : (i + 1) * D] = acc[i].T.astype(bf16)
            pay[3 * D : 4 * D] = dwo2_ref[...]
            dwo1_ref[...] = acc[3].astype(bf16)
            extra[...] = jnp.concatenate(
                [sg_ref[:3], cross_ref[:3], feed_ref[:9], jnp.zeros((1, D), f32)]
            ).astype(bf16)
            if out_plan is None:
                pay[4 * D :] = extra[...]
            deliver(pay, give_refs, out_plan, 64, place_square, sem, extra)

    row_block = pl.BlockSpec((rows, D), lambda i: (i, 0))
    feature = pl.BlockSpec((D, rows), lambda i: (0, i))
    item3 = lambda a, b: pl.BlockSpec((1, a, b), lambda i: (i, 0, 0))
    outs = pl.pallas_call(
        kernel,
        grid=(items,),
        in_specs=[pl.BlockSpec((x.shape[0], rows), lambda i: (0, i)) for x in mixed]
        + [
            feature, item3(D, slots), item3(D, slots), row_block, row_block,
            pl.BlockSpec((rows, 1), lambda i: (i, 0)), item3(slots, D),
            whole((3 * D, D)), whole((D, D)), whole((D, D)), whole((8, D)), whole((16, D)), whole((24, D)),
        ],
        out_specs=[row_block, feature, item3(slots, D), whole((D, D))]
        + [any_spec()] * m,
        out_shape=[
            sds((total, D), bf16), sds((D, total), bf16), sds((items, slots, D), f32),
            sds((D, D), bf16),
        ]
        + out_pieces,
        scratch_shapes=[
            pltpu.VMEM((4, D, D), f32),
            pltpu.VMEM((8, D), f32),
            pltpu.VMEM((4 * D + (SMALL if out_plan is None else 0), D), bf16),
            pltpu.VMEM((SMALL, D), bf16),
            pltpu.SemaphoreType.DMA,
        ],
        compiler_params=params(56),
        cost_estimate=cost(8 * total * D * D, 20e6),
        name="between_backward",
    )(*mixed, dq, dk, dv, ds2, n1, i1, memory, wt2, wo1, dwo2, sg_cross, sg_feed, small)
    return outs[:4], outs[4:]


def self_backward(first, pairs, q, k, v, e, l, o, do1, tau, items, rows):
    total = items * rows
    blocks = rows // QB
    count = block_start(blocks)
    heads = 2 * pairs
    width = heads * HD

    def kernel(
        q_ref, k_ref, v_ref, e_ref, l_ref, o_ref, do_ref, tau_ref, d_ref, tau_out,
        vaug, daug, dks, dvs,
    ):
        item = pl.program_id(0)
        factor = tau_ref[item] * (1.0 / math.sqrt(HD))
        sums = [jnp.zeros((HD, QB), f32)]
        which = lax.broadcasted_iota(jnp.int32, (16, rows), 0)
        for h in range(heads):
            span = slice(h * HD, (h + 1) * HD)
            scaled = (do_ref[span].astype(f32) * l_ref[h // 2, h % 2 : h % 2 + 1]).astype(bf16)
            row_term = -jnp.sum(scaled.astype(f32) * o_ref[span].astype(f32), axis=0, keepdims=True)
            high = row_term.astype(bf16).astype(f32)
            extra = jnp.where(which == 0, high, jnp.where(which == 1, row_term - high, 0.0))
            daug[h, :HD] = scaled
            daug[h, HD:] = extra.astype(bf16)
            vaug[h, :HD] = v_ref[span]
            vaug[h, HD:] = jnp.ones((16, rows), bf16)

        def slope_of(unit, _):
            h, j = unit
            return tn(vaug[h, :, : (j + 1) * QB], daug[h, :, j * QB : (j + 1) * QB])

        def weigh(unit, slope):
            h, j = unit
            at = block_start(j)
            weight = e_ref[0, h, at : at + j + 1].reshape((j + 1) * QB, QB)
            return (weight.astype(f32) * slope).astype(bf16)

        def mix(unit, ds):
            h, j = unit
            span = slice(h * HD, (h + 1) * HD)
            here = slice(j * QB, (j + 1) * QB)
            before, upto = j * QB, (j + 1) * QB
            at = block_start(j)
            weight = e_ref[0, h, at : at + j + 1].reshape(upto, QB)
            raw = nn(k_ref[span, :upto], ds)
            queries = q_ref[span, here]
            sums[0] = sums[0] + raw * queries.astype(f32)
            d_ref[0, span, here] = (raw * factor).astype(bf16)
            dk = nt(queries, ds)
            dv = nt(daug[h, :HD, here], weight)
            if j:
                dks[h, :, :before] += dk[:, :before]
                dvs[h, :, :before] += dv[:, :before]
            dks[h, :, before:upto] = dk[:, before:]
            dvs[h, :, before:upto] = dv[:, before:]

        units = [(h, j) for j in range(blocks) for h in range(heads)]
        pipeline(units, (0, slope_of), (2, weigh), (3, mix))
        for h in range(heads):
            span = slice(h * HD, (h + 1) * HD)
            d_ref[1, span] = (dks[h] * LN2).astype(bf16)
            d_ref[2, span] = dvs[h].astype(bf16)
        tau_sum = sums[0]
        tau_out[0] = jnp.sum(tau_sum, axis=0, keepdims=True)

    feature = pl.BlockSpec((width, rows), lambda i: (first // pairs, i))
    local = pl.BlockSpec((width, rows), lambda i: (0, i))
    return pl.pallas_call(
        kernel,
        grid=(items,),
        in_specs=[
            feature, feature, feature,
            pl.BlockSpec((1, 2 * pairs, count, QB, QB), lambda i: (i, 0, 0, 0, 0)),
            pl.BlockSpec((pairs, 8, rows), lambda i: (0, 0, i)), local, feature, smem(),
        ],
        out_specs=[
            pl.BlockSpec((3, width, rows), lambda i: (0, 0, i)),
            pl.BlockSpec((1, 1, QB), lambda i: (i, 0, 0)),
        ],
        out_shape=[sds((3, width, total), bf16), sds((items, 1, QB), f32)],
        scratch_shapes=[
            pltpu.VMEM((heads, HD + 16, rows), bf16),
            pltpu.VMEM((heads, HD + 16, rows), bf16),
            pltpu.VMEM((heads, HD, rows), f32),
            pltpu.VMEM((heads, HD, rows), f32),
        ],
        compiler_params=params(56),
        cost_estimate=cost(4 * 4 * pairs * items * 2 * rows * rows * 2 * HD, 12e6),
        name="self_backward",
    )(q, k, v, in_hbm(e), l, o, do1, tau)


def self_weight_grad(x, parts, dwo1, out_plan):
    total = x.shape[0]
    n = len(parts)
    out_pieces = piece_shapes(out_plan, 64, 4 * D, SMALL)
    m = len(out_pieces)

    def kernel(*refs):
        part_refs = refs[:n]
        x_ref, dwo_ref = refs[n : n + 2]
        give_refs = refs[n + 2 : n + 2 + m]
        pay, extra, biases, sem = refs[n + 2 + m :]
        which = pl.program_id(0)
        grads = jnp.concatenate([ref[0] for ref in part_refs], axis=0)
        pay[pl.ds(pl.multiple_of(which * D, D), D)] = nn(grads, x_ref[...]).T.astype(bf16)
        biases[which] = nt(jnp.ones((8, total), bf16), grads)

        @pl.when(which == 2)
        def _():
            pay[3 * D : 4 * D] = dwo_ref[...]
            extra[...] = jnp.concatenate(
                [biases[0, :1], biases[2, :1], jnp.zeros((SMALL - 2, D), f32)]
            ).astype(bf16)
            if out_plan is None:
                pay[4 * D :] = extra[...]
            deliver(pay, give_refs, out_plan, 64, place_square, sem, extra)

    return pl.pallas_call(
        kernel,
        grid=(3,),
        in_specs=[pl.BlockSpec((1, p.shape[1], total), lambda i: (i, 0, 0)) for p in parts]
        + [whole((total, D)), whole((D, D))],
        out_specs=[any_spec()] * m,
        out_shape=out_pieces,
        scratch_shapes=[
            pltpu.VMEM((4 * D + (SMALL if out_plan is None else 0), D), bf16),
            pltpu.VMEM((SMALL, D), bf16),
            pltpu.VMEM((3, 8, D), f32),
            pltpu.SemaphoreType.DMA,
        ],
        compiler_params=params(56),
        cost_estimate=cost(6 * total * D * D, 10e6),
        name="self_weight_grad",
    )(*parts, x, dwo1)


def input_grad(ds1, parts, wt):
    n = len(parts)
    total = ds1.shape[0]

    def kernel(*refs):
        part_refs = refs[:n]
        ds1_ref, wt_ref, out_ref = refs[n:]
        grads = jnp.concatenate([ref[i] for i in range(3) for ref in part_refs], axis=0)
        out_ref[...] = ds1_ref[...].astype(f32) + tn(grads, wt_ref[...])

    return pl.pallas_call(
        kernel,
        grid=(total // ROWS,),
        in_specs=[pl.BlockSpec((3, p.shape[1], ROWS), lambda i: (0, 0, i)) for p in parts]
        + [pl.BlockSpec((ROWS, D), lambda i: (i, 0)), whole((3 * D, D))],
        out_specs=pl.BlockSpec((ROWS, D), lambda i: (i, 0)),
        out_shape=sds((total, D), f32),
        compiler_params=params(56),
        cost_estimate=cost(6 * total * D * D, 14e6),
        name="input_grad",
    )(*parts, ds1, wt)


def per_device(
    inputs,
    memory,
    tau_scale,
    delta_shift,
    horizon,
    memory_mask,
    cotangent,
    self_weights,
    cross_weights,
    feed_weights,
    small_params,
):
    items, rows = inputs.shape[0], inputs.shape[1]
    x = inputs.reshape(items * rows, D)
    direct = special()
    in_plan = GATHER_PLAN if direct else None
    out_plan = SCATTER_PLAN if direct else None
    if direct:
        is_up = lax.axis_index("wide") < 8
        width = small_params.shape[0]
        small = lax.dynamic_update_slice(
            jnp.zeros((width * 32,), bf16), small_params, (my_index() * width,)
        ).reshape(17, D)
        held = jnp.concatenate([self_weights.reshape(64, D), pad_rows(small[:2])])
        held, feed_weights, cross_weights = lax.optimization_barrier(
            (held, feed_weights, cross_weights)
        )
        held = join(gather_column(held), SMALL)
        up = feed_weights.reshape(32, 4, D).transpose(1, 0, 2).reshape(128, D)
        own_feed = jnp.where(is_up, up, feed_weights.reshape(128, D))
        held = gather_stage(held, 1, SMALL)
        top = core_hop(held, 0)
        crossed = jnp.concatenate([cross_weights.reshape(64, D), pad_rows(small[2:])])
        swapped = swap(held)
        crossed = join(gather_column(after(crossed, swapped)), SMALL)
        self_pieces = [held, top, swapped, swap(after(top, crossed))]
        crossed, own_feed, _ = lax.optimization_barrier((crossed, own_feed, self_pieces[3]))
        cross_came = core_hop(crossed, 1)
        fed = gather_column(own_feed)
    else:
        small = lax.all_gather(small_params, W, axis=0, tiled=True).reshape(17, D)
        full = lax.all_gather(self_weights, W, axis=0, tiled=True).reshape(4 * D, D)
        self_pieces = [jnp.concatenate([full, pad_rows(small[:2])])]
        full = lax.all_gather(cross_weights, W, axis=0, tiled=True).reshape(4 * D, D)
        cross_pieces = [jnp.concatenate([full, pad_rows(small[2:])])]
        full = lax.all_gather(feed_weights, W, axis=0, tiled=True)
        up = full[: D * FF].reshape(16, 32, 4, D).transpose(0, 2, 1, 3).reshape(4 * D, D)
        feed_pieces = [jnp.concatenate([up, full[D * FF :].reshape(4 * D, D)])]

    q1, k1, v1, wt1, wo1 = project_self(x, self_pieces, in_plan, tau_scale)
    if direct:
        cross_came, q1 = lax.optimization_barrier((cross_came, q1))
        crossed = join([crossed, cross_came], SMALL)
        cross_came = core_hop(crossed, 0)
        q1 = after(q1, crossed)
    first = 0
    kept = []
    for pairs in GROUPS:
        if kept:
            q1 = after(q1, kept[-1][3])
            if direct:
                *fed, cross_came, o1 = lax.optimization_barrier((*fed, cross_came, kept[-1][3]))
                kept[-1] = kept[-1][:3] + (o1,) + kept[-1][4:]
                fed = join(fed)
                feed_came = core_hop(fed, 1)
                cross_pieces = [crossed, cross_came, swap(crossed), swap(cross_came)]
                q1 = after(q1, fed, cross_came)
        kept.append((first, pairs) + tuple(attend_self(first, pairs, q1, k1, v1, items, rows)))
        first += pairs
    if direct:
        feed_came, wo1, *swapped = lax.optimization_barrier(
            (feed_came, wo1, *cross_pieces[2:], kept[-1][3])
        )
        cross_pieces[2:] = swapped[:2]
        fed = join([fed, feed_came])
        feed_came = core_hop(fed, 0)
        feed_pieces = [fed, feed_came, swap(fed)]
        wo1 = after(wo1, fed)
    mixed = [group[3] for group in kept]
    n1, i1, n2, i2, q2, k2, v2, e2, l2, o2, wt2, wo2, small = cross_forward(
        x, mixed, wo1, cross_pieces, in_plan, tau_scale, memory, delta_shift, memory_mask
    )
    if direct:
        feed_pieces.append(swap(after(feed_came, n2)))
    output, ds2, sg_feed, feed_give = feed(
        n2, i2, feed_pieces, in_plan, out_plan, small, horizon,
        cotangent.reshape(items * rows, D), rows,
    )
    if direct:
        feed_steps = Scatter(*feed_give, 128)
    dq2, dk2, dv2, tau_two, shift_sum, dwo2, sg_cross = cross_backward(
        ds2, q2, k2, v2, e2, l2, o2, wo2, tau_scale, items, rows
    )
    if direct:
        feed_steps.wait(dq2)
        dq2 = after(dq2, feed_steps.first())
    (ds1, do1, grad_memory, dwo1), cross_give = between_backward(
        dq2, dk2, dv2, ds2, n1, i1, mixed, memory, wt2, wo1, dwo2, sg_cross, sg_feed, out_plan,
        small, items, rows,
    )
    if direct:
        cross_steps = Scatter(*cross_give, 64, SMALL)
        feed_steps.wait(do1)
        do1 = after(do1, feed_steps.second())
    parts, taus = [], []
    for first, pairs, e1, o1, l1 in kept:
        if len(parts) == 1:
            do1 = after(do1, parts[0])
            if direct:
                feed_steps.wait(parts[0])
                cross_steps.wait(parts[0])
                do1 = after(do1, feed_steps.column(), cross_steps.first())
        part, tau_one = self_backward(
            first, pairs, q1, k1, v1, e1, l1, o1, do1, tau_scale, items, rows
        )
        parts.append(part)
        taus.append(tau_one)
    if direct:
        cross_steps.wait(parts[-1])
        dwo1 = after(dwo1, cross_steps.second(), *feed_steps.came[1:])
    self_give = self_weight_grad(x, parts, dwo1, out_plan)
    if direct:
        keep, send = self_give
        self_steps = Scatter(keep, after(send, cross_steps.came), 64, SMALL)
        feed_steps.wait_column(keep)
        tau_two, shift_sum, taus, _ = lax.optimization_barrier((tau_two, shift_sum, taus, keep))
    grad_tau = sum(jnp.sum(t, axis=(1, 2)) for t in [tau_two] + taus) / (LOG2E * tau_scale)
    grad_delta = shift_sum[:, :, 0]
    if direct:
        (own_feed,) = feed_steps.total()
        up = own_feed.reshape(4, 32, D).transpose(1, 0, 2).reshape(-1)
        grad_feed = jnp.where(is_up, up, own_feed.reshape(-1))
        self_steps.wait(grad_feed, grad_tau, grad_delta)
        ds1 = after(ds1, self_steps.first())
    grad_inputs = input_grad(ds1, parts, wt1)
    if direct:
        self_steps.wait(grad_inputs)
        sent = self_steps.second()
        cross_steps.wait(sent)
        cross_steps.column()
        last = self_steps.column()
        cross_steps.wait_column(last)

    if direct:
        grad_cross, small_rest = cross_steps.total()
        grad_self, small_grad = self_steps.total()
        grad_self = grad_self.reshape(-1)
        grad_cross = grad_cross.reshape(-1)
        small_grad = jnp.concatenate([small_grad[:2], small_rest[:15]]).reshape(-1)
        grad_small = lax.dynamic_slice(small_grad, (my_index() * width,), (width,))
    else:
        scatter = lambda v: lax.psum_scatter(v.reshape(-1), W, scatter_dimension=0, tiled=True)
        full, rest = self_give[0].astype(f32), cross_give[0].astype(f32)
        grad_self, grad_cross = scatter(full[: 4 * D]), scatter(rest[: 4 * D])
        small_grad = jnp.concatenate([full[4 * D : 4 * D + 2], rest[4 * D : 4 * D + 15]])
        grad_small = scatter(small_grad)
        full = feed_give[0].astype(f32)
        up = full[: 4 * D].reshape(16, 4, 32, D).transpose(0, 2, 1, 3).reshape(-1)
        grad_feed = scatter(jnp.concatenate([up, full[4 * D :].reshape(-1)]))
    return (
        output.reshape(items, rows, D),
        grad_inputs.reshape(items, rows, D),
        grad_memory,
        grad_tau,
        grad_delta,
        grad_self,
        grad_cross,
        grad_feed,
        grad_small,
    )


def solution(mesh):
    whole_mesh = P(W)
    rows3 = P(W, None, None)
    rows2 = P(W, None)
    return jax.shard_map(
        per_device,
        mesh=mesh,
        in_specs=(
            rows3, rows3, whole_mesh, rows2, whole_mesh, rows2, rows3,
            whole_mesh, whole_mesh, whole_mesh, whole_mesh,
        ),
        out_specs=(
            rows3, rows3, rows3, whole_mesh, rows2, whole_mesh, whole_mesh, whole_mesh, whole_mesh,
        ),
        check_vma=False,
    )
```

```python
import math

import jax
import jax.numpy as jnp
from jax import lax
from jax.experimental import pallas as pl
from jax.experimental.pallas import tpu as pltpu
from jax.sharding import PartitionSpec as P

D = 512
H = 8
HD = 64
FF = 2048
LABEL = 48
EPS = 1e-05
LOG2E = math.log2(math.e)
LN2 = math.log(2.0)
MASKED = -1e30 * LOG2E
QB = 256
GROUPS = (2, 2)
FEED_ROWS = 512
FEED_SUBS = 2
ROWS = 768
W = ("wide", "narrow")
SMALL = 16
bf16 = jnp.bfloat16
f32 = jnp.float32


def nn(a, b):
    return lax.dot_general(a, b, (((1,), (0,)), ((), ())), preferred_element_type=f32)


def nt(a, b):
    return lax.dot_general(a, b, (((1,), (1,)), ((), ())), preferred_element_type=f32)


def tn(a, b):
    return lax.dot_general(a, b, (((0,), (0,)), ((), ())), preferred_element_type=f32)


def upright(row):
    return jnp.broadcast_to(row, (128, row.shape[1])).T[:, :1]


def any_spec():
    return pl.BlockSpec(memory_space=pl.ANY)


def whole(shape):
    return pl.BlockSpec(shape, lambda *_: (0,) * len(shape))


def smem():
    return pl.BlockSpec(memory_space=pltpu.SMEM)


def params(mib):
    return pltpu.CompilerParams(
        vmem_limit_bytes=mib * 1024 * 1024, dimension_semantics=("arbitrary",)
    )


def cost(flops, nbytes, trans=0):
    return pl.CostEstimate(flops=int(flops), bytes_accessed=int(nbytes), transcendentals=int(trans))


def in_hbm(v):
    return pltpu.with_memory_space_constraint(v, pltpu.HBM)


def sds(shape, dtype):
    return jax.ShapeDtypeStruct(shape, dtype)


def place_square(s):
    return [(0, 64, 64 * s)]


def my_index():
    return lax.axis_index("wide") * 2 + lax.axis_index("narrow")


def aligned(row):
    return row if isinstance(row, int) else pl.multiple_of(row, 32)


def fetch(refs, plan, unit, place, dst, sem, extra=None):
    if plan is None:
        pltpu.make_async_copy(refs[0], dst, sem).start()
    else:
        for ref, held in zip(refs, plan):
            for i, (piece, other) in enumerate(held):
                for src, size, row in place(piece_owners(piece, other)):
                    pltpu.make_async_copy(
                        ref.at[pl.ds(i * unit + src, size)],
                        dst.at[pl.ds(aligned(row), size)],
                        sem,
                    ).start()
        if extra is not None:
            for k, (ref, held) in enumerate(zip(refs, plan)):
                pltpu.make_async_copy(
                    ref.at[pl.ds(len(held) * unit, SMALL)], extra.at[pl.ds(k * SMALL, SMALL)], sem
                ).start()
            pltpu.make_async_copy(extra, extra, sem).wait()
    pltpu.make_async_copy(dst, dst, sem).wait()


def deliver(src, refs, plan, unit, place, sem, extra=None, stepped=False):
    if plan is None:
        pltpu.make_async_copy(src, refs[0], sem).start()
    else:
        for ref, held in zip(refs, plan):
            for i, (piece, other) in enumerate(held):
                for dst, size, row in place(piece_owners(piece, other, stepped)):
                    pltpu.make_async_copy(
                        src.at[pl.ds(aligned(row), size)],
                        ref.at[pl.ds(i * unit + dst, size)],
                        sem,
                    ).start()
        if extra is not None:
            for ref, held in zip(refs, plan):
                pltpu.make_async_copy(extra, ref.at[pl.ds(len(held) * unit, SMALL)], sem).start()
            for _ in refs:
                pltpu.make_async_copy(extra, extra, sem).wait()
    pltpu.make_async_copy(src, src, sem).wait()


def fetch_blocks(refs, plan, dst, sem):
    if plan is None:
        pltpu.make_async_copy(refs[0], dst, sem).start()
    else:
        for ref, held in zip(refs, plan):
            for i, (piece, other) in enumerate(held):
                owner = piece_owners(piece, other, True)
                pltpu.make_async_copy(ref.at[i], dst.at[owner], sem).start()
    pltpu.make_async_copy(dst, dst, sem).wait()


def deliver_blocks(src, refs, plan, sem, first_half):
    half = src.shape[0] // 2
    here = slice(0, half) if first_half else slice(half, 2 * half)
    if plan is None:
        pltpu.make_async_copy(src.at[here], refs[0].at[here], sem).start()
        return
    for ref, held in zip(refs, plan):
        for i, (piece, other) in enumerate(held):
            owner = piece_owners(piece, other)

            @pl.when((owner < half) if first_half else (owner >= half))
            def _():
                pltpu.make_async_copy(src.at[owner], ref.at[i], sem).start()


def swap(v):
    return lax.ppermute(v, "narrow", [(0, 1), (1, 0)])


def special():
    return lax.axis_size("wide") == 16 and lax.axis_size("narrow") == 2


CORE_MASKS = ((1, 2), (2, 1))
COLUMN = (0, 4, 8, 12)


def core_hop(v, stage):
    n = lax.axis_size("wide")
    return lax.ppermute(
        v, W, [(2 * i + c, 2 * (i ^ CORE_MASKS[c][stage]) + c) for i in range(n) for c in range(2)]
    )


def column_hop(v, mask):
    n = lax.axis_size("wide")
    return lax.ppermute(v, "wide", [(i, i ^ mask) for i in range(n)])


COLUMN_STEPS = ((4, 8), (8, 4))


def column_step(v, step):
    n = lax.axis_size("wide")
    return lax.ppermute(
        v, W, [(2 * i + c, 2 * (i ^ COLUMN_STEPS[c][step]) + c) for i in range(n) for c in range(2)]
    )


def masks_of(core):
    return [jnp.where(core == 0, a, b) for a, b in zip(*CORE_MASKS)]


def wide_mask(q, masks, column):
    total = column
    for bit, mask in zip((8, 4), masks):
        if q & bit:
            total = total + mask
    return total


def piece_owners(q, other, stepped=False):
    core = lax.axis_index("narrow")
    wide = lax.axis_index("wide")
    core = 1 - core if other else core
    column = COLUMN[q % 4]
    if stepped:
        column = jnp.where(core == 0, column, (0, 8, 4, 12)[q % 4])
    return (wide ^ wide_mask(q, masks_of(core), column)) * 2 + core


GATHER_PLAN = tuple(
    tuple((q, other) for q in qs)
    for other in (False, True)
    for qs in ((0, 1, 2, 3, 4, 5, 6, 7), (8, 9, 10, 11, 12, 13, 14, 15))
)
SCATTER_PLAN = tuple(tuple((q, other) for q in range(16)) for other in (False, True))


def after(v, *others):
    return lax.optimization_barrier((v,) + others)[0]


def pad_rows(v):
    return jnp.pad(v, ((0, SMALL - v.shape[0]), (0, 0)))


def join(parts, extra=0):
    if not extra:
        return jnp.concatenate(parts)
    n = parts[0].shape[0] - extra
    return jnp.concatenate([p[:n] for p in parts] + [sum(p[n:] for p in parts[1:]) + parts[0][n:]])


def gather_column(own):
    far = [column_hop(own, mask) for mask in COLUMN[:0:-1]]
    return [own] + far[::-1]


def gather_stage(held, stage, extra=0):
    return join([held, core_hop(held, stage)], extra)


def add(*terms):
    total = terms[0].astype(f32)
    for term in terms[1:]:
        total = total + term.astype(f32)
    return total


def fold(arrays, outputs):
    n = len(arrays)

    def kernel(*refs):
        for out, (dtype, segments) in zip(refs[n:], outputs):
            at = 0
            for height, terms in segments:
                total = add(*[refs[i][first : first + height] for i, first in terms])
                out[at : at + height] = total.astype(dtype)
                at += height

    in_vmem = pl.BlockSpec(memory_space=pltpu.VMEM)
    shapes = [sds((sum(h for h, _ in segments), D), dtype) for dtype, segments in outputs]
    return pl.pallas_call(
        kernel,
        in_specs=[in_vmem] * n,
        out_specs=[in_vmem] * len(outputs),
        out_shape=shapes,
        compiler_params=pltpu.CompilerParams(vmem_limit_bytes=16 * 1024 * 1024),
        cost_estimate=cost(1e6, sum(v.size * 2 for v in arrays)),
        name="fold",
    )(*arrays)


class Scatter:
    def __init__(self, keep, send, unit, extra=0):
        self.unit, self.extra = unit, extra
        self.keep, self.came = keep, swap(send)

    def wait(self, *others):
        self.came = after(self.came, *others)

    def first(self):
        half = 8 * self.unit
        if self.extra:
            (self.sent,) = fold(
                [self.keep, self.came], [(bf16, [(half + self.extra, [(0, half), (1, half)])])]
            )
            self.kept = [self.keep, self.came]
        else:
            self.sent = add(self.keep[half:], self.came[half:]).astype(bf16)
            self.kept = [add(self.keep[:half], self.came[:half]).astype(bf16)]
        self.came = core_hop(self.sent, 0)
        return self.sent

    def second(self):
        half, n = 4 * self.unit, len(self.kept)
        sent = [(half, [(i, half) for i in range(n + 1)])]
        if self.extra:
            sent.append((self.extra, [(n, 2 * half), (n + 1, 2 * half)]))
        self.sent, self.kept = fold(
            self.kept + [self.came, self.sent],
            [(bf16, sent), (f32, [(half, [(i, 0) for i in range(n + 1)])])],
        )
        self.came = core_hop(self.sent, 1)
        return self.sent

    def column(self):
        unit = self.unit
        outputs = [(f32, [(unit, [(0, 0), (1, 0)])])]
        for z in range(1, 4):
            outputs.append((bf16, [(unit, [(0, z * unit), (1, z * unit)])]))
            if self.extra:
                outputs[z][1].append((self.extra, [(1, 4 * unit), (2, 4 * unit)]))
        outs = fold([self.kept, self.came, self.sent], outputs)
        self.kept, self.sent = outs[0], outs[1]
        self.came = [None] + [column_hop(v, COLUMN[z]) for z, v in zip((3, 2, 1), outs[:0:-1])]
        return outs[3]

    def column_one(self):
        half = 2 * self.unit
        self.sent, self.kept = fold(
            [self.kept, self.came, self.sent],
            [
                (bf16, [(half, [(0, half), (1, half)]), (self.extra, [(1, 2 * half), (2, 2 * half)])]),
                (f32, [(half, [(0, 0), (1, 0)])]),
            ],
        )
        self.came = column_step(self.sent, 1)
        return self.sent

    def column_two(self):
        unit = self.unit
        self.sent, self.kept = fold(
            [self.kept, self.came, self.sent],
            [
                (bf16, [(unit, [(0, unit), (1, unit)]), (self.extra, [(1, 2 * unit), (2, 2 * unit)])]),
                (f32, [(unit, [(0, 0), (1, 0)])]),
            ],
        )
        self.came = column_step(self.sent, 0)
        return self.sent

    def total_two(self):
        unit = self.unit
        return fold(
            [self.kept, self.came, self.sent],
            [(f32, [(unit, [(0, 0), (1, 0)])]), (f32, [(self.extra, [(1, unit), (2, unit)])])],
        )

    def wait_column(self, *others):
        self.came[1:] = lax.optimization_barrier(tuple(self.came[1:]) + others)[:3]

    def total(self):
        outputs = [(f32, [(self.unit, [(i, 0) for i in range(4)])])]
        if self.extra:
            outputs.append((f32, [(self.extra, [(i, self.unit) for i in range(1, 5)])]))
        return fold([self.kept] + self.came[1:] + [self.sent], outputs)


def norm_forward(s):
    centred = s - jnp.mean(s, axis=-1, keepdims=True)
    inverse = lax.rsqrt(jnp.mean(centred * centred, axis=-1, keepdims=True) + EPS)
    return centred * inverse, inverse


def norm_backward(grad, normal, inverse, gain):
    scaled = grad * gain
    grad_in = inverse * (
        scaled
        - jnp.mean(scaled, axis=-1, keepdims=True)
        - normal * jnp.mean(scaled * normal, axis=-1, keepdims=True)
    )
    return (
        grad_in,
        jnp.sum(grad * normal, axis=0, keepdims=True),
        jnp.sum(grad, axis=0, keepdims=True),
    )


def gelu_parts(u):
    cumulative = 0.5 + 0.5 * lax.erf(u * math.sqrt(0.5))
    density = jnp.exp2(u * u * (-0.5 * LOG2E)) * (1.0 / math.sqrt(2.0 * math.pi))
    return u * cumulative, cumulative + u * density


def pipeline(units, *stages):
    held = {}
    for turn in range(len(units) + max(delay for delay, _ in stages)):
        for delay, stage in stages:
            at = turn - delay
            if 0 <= at < len(units):
                held[at] = stage(units[at], held.get(at))


def interleave(streams):
    live = list(streams)
    while live:
        live = [stream for stream in live if next(stream, live) is not live]


def small_rows(w, extra, plan):
    if plan is None:
        return w[4 * D :].astype(f32)
    return add(*[extra[k * SMALL : (k + 1) * SMALL] for k in range(extra.shape[0] // SMALL)])


def project_self(x, pieces, plan, tau):
    total = x.shape[0]
    per_item = total // (tau.shape[0] * ROWS)
    n = len(pieces)
    full = 4 * D + SMALL if plan is None else 4 * D

    def kernel(*refs):
        piece_refs = refs[:n]
        x_ref, tau_ref, q_ref, k_ref, v_ref, wt_ref, wo_ref, w, extra, cols, sem = refs[n:]
        step = pl.program_id(0)

        @pl.when(step == 0)
        def _():
            fetch(piece_refs, plan, 64, place_square, w, sem, extra)
            small = small_rows(w, extra, plan)
            cols[0] = upright(small[0:1])
            cols[1] = upright(small[1:2])
            for m in range(3):
                wt_ref[m * D : (m + 1) * D] = w[m * D : (m + 1) * D].T
            wo_ref[...] = w[3 * D : 4 * D]

        factor = tau_ref[lax.div(step, per_item)] * (LOG2E / math.sqrt(HD))
        rows_in = x_ref[...]
        q_ref[...] = ((nt(wt_ref[:D], rows_in) + cols[0]) * factor).astype(bf16)
        k_ref[...] = nt(wt_ref[D : 2 * D], rows_in).astype(bf16)
        v_ref[...] = (nt(wt_ref[2 * D :], rows_in) + cols[1]).astype(bf16)

    feature = pl.BlockSpec((D, ROWS), lambda i: (0, i))
    return pl.pallas_call(
        kernel,
        grid=(total // ROWS,),
        in_specs=[any_spec()] * n
        + [pl.BlockSpec((ROWS, D), lambda i: (i, 0)), smem()],
        out_specs=[feature] * 3 + [whole((3 * D, D)), whole((D, D))],
        out_shape=[sds((D, total), bf16)] * 3
        + [sds((3 * D, D), bf16), sds((D, D), bf16)],
        scratch_shapes=[
            pltpu.VMEM((full, D), bf16),
            pltpu.VMEM((n * SMALL, D), bf16),
            pltpu.VMEM((2, D, 1), f32),
            pltpu.SemaphoreType.DMA,
        ],
        compiler_params=params(56),
        cost_estimate=cost(6 * total * D * D, 12e6),
        name="project_self",
    )(*pieces, x, tau)


def block_start(j):
    return j * (j + 1) // 2


def attend_self(first, pairs, q, k, v, items, rows):
    blocks = rows // QB
    count = block_start(blocks)
    heads = 2 * pairs

    def kernel(q_ref, k_ref, v_ref, e_ref, o_ref, l_ref, vaug):
        key_place = lax.broadcasted_iota(jnp.int32, (QB, QB), 0)
        query_place = lax.broadcasted_iota(jnp.int32, (QB, QB), 1)
        allowed = key_place <= query_place
        for h in range(heads):
            vaug[h, :HD] = v_ref[h * HD : (h + 1) * HD]
            vaug[h, HD:] = jnp.ones((16, rows), bf16)

        def score(unit, _):
            h, j = unit
            span = slice(h * HD, (h + 1) * HD)
            return tn(k_ref[span, : (j + 1) * QB], q_ref[span, j * QB : (j + 1) * QB])

        def weigh(unit, scores):
            h, j = unit
            diagonal = jnp.where(allowed, scores[j * QB :], MASKED)
            top = jnp.max(diagonal, axis=0, keepdims=True)
            if j:
                top = jnp.maximum(top, jnp.max(scores[: j * QB], axis=0, keepdims=True))
            weights = []
            for b in range(j + 1):
                part = diagonal if b == j else scores[b * QB : (b + 1) * QB]
                weight = jnp.exp2(part - top).astype(bf16)
                e_ref[0, h, block_start(j) + b] = weight
                weights.append(weight)
            return jnp.concatenate(weights, axis=0) if j else weights[0]

        def mix(unit, weights):
            h, j = unit
            here = slice(j * QB, (j + 1) * QB)
            mixed = nn(vaug[h, :, : (j + 1) * QB], weights)
            inverse = 1.0 / mixed[HD : HD + 1]
            o_ref[h * HD : (h + 1) * HD, here] = (mixed[:HD] * inverse).astype(bf16)
            l_ref[h // 2, h % 2 : h % 2 + 1, here] = inverse

        units = [(h, j) for j in range(blocks) for h in range(heads)]
        pipeline(units, (0, score), (2, weigh), (3, mix))

    total = items * rows
    height = heads * HD
    feature = pl.BlockSpec((height, rows), lambda i: (first // pairs, i))
    return pl.pallas_call(
        kernel,
        grid=(items,),
        in_specs=[feature] * 3,
        out_specs=[
            pl.BlockSpec((1, heads, count, QB, QB), lambda i: (i, 0, 0, 0, 0)),
            pl.BlockSpec((height, rows), lambda i: (0, i)),
            pl.BlockSpec((pairs, 8, rows), lambda i: (0, 0, i)),
        ],
        out_shape=[
            pltpu.HBM((items, heads, count, QB, QB), bf16),
            sds((height, total), bf16),
            sds((pairs, 8, total), f32),
        ],
        scratch_shapes=[pltpu.VMEM((heads, HD + 16, rows), bf16)],
        compiler_params=params(56),
        cost_estimate=cost(4 * 4 * pairs * items * 2 * rows * rows * HD, 8e6 * pairs / 2),
        name="attend_self",
    )(q, k, v)


def cross_forward(x, mixed, wo1, pieces, plan, tau, memory, shift, mask):
    items, slots = memory.shape[0], memory.shape[1]
    total = x.shape[0]
    rows = total // items
    blocks = rows // ROWS
    n = len(pieces)
    n_mixed = len(mixed)

    def kernel(*refs):
        piece_refs = refs[:n]
        mixed_refs = refs[n : n + n_mixed]
        x_ref, wo1_ref, tau_ref, mem_ref, shift_ref, mask_ref = refs[n + n_mixed : n + n_mixed + 6]
        (
            n1_ref, i1_ref, n2_ref, i2_ref, q_ref, k_ref, v_ref, e_ref, l_ref, o_ref,
            wt_ref, wo2_ref, small_ref, w, extra, cols, vaug, sem,
        ) = refs[n + n_mixed + 6 :]
        step = pl.program_id(0)
        item = lax.div(step, blocks)

        @pl.when(step == 0)
        def _():
            fetch(piece_refs, plan, 64, place_square, w, sem, extra)
            small_ref[2:17] = small_rows(w, extra, plan)[:15]
            cols[0] = upright(small_ref[5:6])
            cols[1] = upright(small_ref[6:7])
            for m in range(3):
                wt_ref[m * D : (m + 1) * D] = w[m * D : (m + 1) * D].T
            wo2_ref[...] = w[3 * D : 4 * D]

        mixed_one = jnp.concatenate([ref[...] for ref in mixed_refs], axis=0)
        summed = x_ref[...].astype(f32) + tn(mixed_one, wo1_ref[...]) + small_ref[2:3]
        normal, inverse = norm_forward(summed)
        n1_ref[...] = normal.astype(bf16)
        i1_ref[...] = inverse
        y1 = normal * small_ref[3:4] + small_ref[4:5]
        y1_low = y1.astype(bf16)
        factor = tau_ref[item] * (LOG2E / math.sqrt(HD))
        q_ref[...] = ((nt(wt_ref[:D], y1_low) + cols[0]) * factor).astype(bf16)

        @pl.when(step == item * blocks)
        def _():
            mem = mem_ref[0]
            k_ref[0] = nt(wt_ref[D : 2 * D], mem).astype(bf16)
            v_ref[0] = (nt(wt_ref[2 * D :], mem) + cols[1]).astype(bf16)
            for h in range(H):
                vaug[h, :HD] = v_ref[0, h * HD : (h + 1) * HD]
                vaug[h, HD:] = jnp.ones((16, slots), bf16)

        bias = upright(shift_ref[pl.ds(item, 1)] * LOG2E)
        allowed = upright(mask_ref[pl.ds(item, 1)].astype(f32)) == 1.0

        def score(h, _):
            span = slice(h * HD, (h + 1) * HD)
            return tn(k_ref[0, span], q_ref[span])

        def weigh(h, scores):
            scores = jnp.where(allowed, scores + bias, MASKED)
            top = jnp.max(scores, axis=0, keepdims=True)
            weight = jnp.exp2(scores - top).astype(bf16)
            e_ref[0, h] = weight
            return weight

        def mix(h, weight):
            got = nn(vaug[h], weight)
            inv = 1.0 / got[HD : HD + 1]
            l_ref[0, h : h + 1] = inv
            o_ref[h * HD : (h + 1) * HD] = (got[:HD] * inv).astype(bf16)

        pipeline(range(H), (0, score), (2, weigh), (3, mix))
        summed = y1 + tn(o_ref[...], wo2_ref[...]) + small_ref[7:8]
        normal, inverse = norm_forward(summed)
        n2_ref[...] = normal.astype(bf16)
        i2_ref[...] = inverse

    row_block = pl.BlockSpec((ROWS, D), lambda i: (i, 0))
    thin = pl.BlockSpec((ROWS, 1), lambda i: (i, 0))
    feature = pl.BlockSpec((D, ROWS), lambda i: (0, i))
    item3 = lambda a, b: pl.BlockSpec((1, a, b), lambda i: (i // blocks, 0, 0))
    return pl.pallas_call(
        kernel,
        grid=(total // ROWS,),
        in_specs=[any_spec()] * n
        + [pl.BlockSpec((m.shape[0], ROWS), lambda i: (0, i)) for m in mixed]
        + [row_block, whole((D, D)), smem(), item3(slots, D),
           whole((items, slots)), whole((items, slots))],
        out_specs=[
            row_block, thin, row_block, thin, feature, item3(D, slots), item3(D, slots),
            pl.BlockSpec((1, H, slots, ROWS), lambda i: (i // blocks, 0, 0, i % blocks)),
            pl.BlockSpec((1, H, ROWS), lambda i: (i // blocks, 0, i % blocks)), feature,
            whole((3 * D, D)), whole((D, D)), whole((24, D)),
        ],
        out_shape=[
            sds((total, D), bf16), sds((total, 1), f32),
            sds((total, D), bf16), sds((total, 1), f32), sds((D, total), bf16),
            sds((items, D, slots), bf16), sds((items, D, slots), bf16),
            sds((items, H, slots, rows), bf16), sds((items, H, rows), f32), sds((D, total), bf16),
            sds((3 * D, D), bf16), sds((D, D), bf16), sds((24, D), f32),
        ],
        scratch_shapes=[
            pltpu.VMEM((4 * D + (SMALL if plan is None else 0), D), bf16),
            pltpu.VMEM((n * SMALL, D), bf16),
            pltpu.VMEM((2, D, 1), f32),
            pltpu.VMEM((H, HD + 16, slots), bf16),
            pltpu.SemaphoreType.DMA,
        ],
        compiler_params=params(56),
        cost_estimate=cost(9 * total * D * D, 20e6),
        name="cross_forward",
    )(*pieces, *mixed, x, wo1, tau, memory, shift, mask)


def piece_shapes(plan, rows, full_rows, extra=0):
    if plan is None:
        return [sds((full_rows + extra, D), bf16)]
    return [sds((len(held) * rows + extra, D), bf16) for held in plan]


def feed(n2, i2, pieces, plan, out_plan, small, horizon, cotangent, rows):
    total = n2.shape[0]
    block = FEED_ROWS
    subs = FEED_SUBS
    size = block // subs
    steps = total // block
    per_item = rows // size
    out_pieces = [sds((32 if out_plan is None else len(h), 4, 32, D), bf16) for h in out_plan or [()]]
    m = len(out_pieces)
    n = len(pieces)

    def kernel(*refs):
        piece_refs = refs[:n]
        n2_ref, i2_ref, small_ref, horizon_ref, cot_ref = refs[n : n + 5]
        out_ref, ds2_ref, sg_ref = refs[n + 5 : n + 8]
        give_refs = refs[n + 8 : n + 8 + m]
        w_ref, acts, grads, y2s, dzs, slopes, pay, sem = refs[n + 8 + m :]
        step = pl.program_id(0)

        @pl.when(step == 0)
        def _():
            fetch_blocks(piece_refs, plan, w_ref, sem)
            sg_ref[...] = jnp.zeros_like(sg_ref)

        def up(c):
            return w_ref[:16, c].reshape(D, D)

        def down(c):
            return w_ref[16 + 4 * c : 20 + 4 * c].reshape(D, D)

        def one(sub):
            local = slice(sub * size, (sub + 1) * size)
            here = pl.ds(pl.multiple_of(step * block + sub * size, size), size)
            n2 = n2_ref[local].astype(f32)
            y2 = n2 * small_ref[8:9] + small_ref[9:10]
            y2_low = y2.astype(bf16)
            y2s[here] = y2_low
            ahead = nn(y2_low, up(0))
            yield
            summed = y2 + small_ref[14:15]
            for c in range(4):
                cols = slice(c * D, (c + 1) * D)
                hidden = ahead + small_ref[10 + c : 11 + c]
                if c < 3:
                    ahead = nn(y2_low, up(c + 1))
                act, slope = gelu_parts(hidden)
                slopes[sub, c] = slope
                act = act.astype(bf16)
                acts[here, cols] = act
                yield
                summed = summed + nn(act, down(c))
                yield
            normal, inverse = norm_forward(summed)
            position = step * subs + sub
            item = lax.div(position, per_item)
            place = (position - item * per_item) * size
            place = place + lax.broadcasted_iota(jnp.int32, (size, 1), 0)
            valid = place < LABEL + horizon_ref[item]
            gain = small_ref[15:16]
            out_ref[local] = jnp.where(valid, normal * gain + small_ref[16:17], 0.0).astype(bf16)
            yield
            grad = jnp.where(valid, cot_ref[local].astype(f32), 0.0)
            ds3, dg3, dc3 = norm_backward(grad, normal, inverse, gain)
            dz = ds3.astype(bf16)
            dzs[here] = dz
            sg_ref[6:7] += jnp.sum(dz.astype(f32), axis=0, keepdims=True)
            sg_ref[7:8] += dg3
            sg_ref[8:9] += dc3
            yield
            dy2 = ds3
            ahead = nt(dz, down(0))
            yield
            for c in range(4):
                du = ahead * slopes[sub, c]
                if c < 3:
                    ahead = nt(dz, down(c + 1))
                du = du.astype(bf16)
                grads[here, c * D : (c + 1) * D] = du
                sg_ref[2 + c : 3 + c] += jnp.sum(du.astype(f32), axis=0, keepdims=True)
                yield
                dy2 = dy2 + nt(du, up(c))
                yield
            ds2, dg2, dc2 = norm_backward(dy2, n2, i2_ref[local], small_ref[8:9])
            ds2_ref[local] = ds2.astype(bf16)
            sg_ref[0:1] += dg2
            sg_ref[1:2] += dc2
            yield

        interleave([one(sub) for sub in range(subs)])

        @pl.when(step == steps - 1)
        def _():
            pay[16:] = tn(acts[...], dzs[...]).astype(bf16).reshape(16, 4, 32, D)
            deliver_blocks(pay, give_refs, out_plan, sem, False)
            grad = tn(y2s[...], grads[...]).astype(bf16)
            for c in range(4):
                pay[:16, c] = grad[:, c * D : (c + 1) * D].reshape(16, 32, D)
            deliver_blocks(pay, give_refs, out_plan, sem, True)
            pltpu.make_async_copy(pay, pay, sem).wait()

    row_block = pl.BlockSpec((block, D), lambda i: (i, 0))
    outs = pl.pallas_call(
        kernel,
        grid=(steps,),
        in_specs=[any_spec()] * n
        + [
            row_block, pl.BlockSpec((block, 1), lambda i: (i, 0)), whole((24, D)), smem(), row_block,
        ],
        out_specs=[row_block, row_block, whole((16, D))] + [any_spec()] * m,
        out_shape=[sds((total, D), bf16), sds((total, D), bf16), sds((16, D), f32)] + out_pieces,
        scratch_shapes=[
            pltpu.VMEM((32, 4, 32, D), bf16),
            pltpu.VMEM((total, FF), bf16),
            pltpu.VMEM((total, FF), bf16),
            pltpu.VMEM((total, D), bf16),
            pltpu.VMEM((total, D), bf16),
            pltpu.VMEM((subs, 4, size, D), f32),
            pltpu.VMEM((32, 4, 32, D), bf16),
            pltpu.SemaphoreType.DMA,
        ],
        compiler_params=params(56),
        cost_estimate=cost(12 * total * D * FF, 20e6),
        name="feed",
    )(*[v.reshape(-1, 4, 32, D) for v in pieces], n2, i2, small, horizon, cotangent)
    return outs[0], outs[1], outs[2], [v.reshape(-1, D) for v in outs[3:]]


def cross_backward(ds2, q, k, v, e, l, o, wo2, tau, items, rows):
    total = items * rows
    slots = k.shape[2]

    def kernel(
        ds2_ref, q_ref, k_ref, v_ref, e_ref, l_ref, o_ref, wo2_ref, tau_ref,
        dq_ref, dk_ref, dv_ref, tau_out, shift_out, dwo2_ref, sg_ref, acc, do2,
    ):
        item = pl.program_id(0)

        @pl.when(item == 0)
        def _():
            acc[...] = jnp.zeros_like(acc)
            sg_ref[...] = jnp.zeros_like(sg_ref)

        da2 = ds2_ref[...]
        do2[...] = nt(wo2_ref[...], da2)
        factor = tau_ref[item] * (1.0 / math.sqrt(HD))
        sums = [jnp.zeros((slots, rows), f32), jnp.zeros((HD, rows), f32)]

        def spread(h, _):
            span = slice(h * HD, (h + 1) * HD)
            scaled = (do2[span].astype(bf16).astype(f32) * l_ref[0, h : h + 1]).astype(bf16)
            row_term = jnp.sum(scaled.astype(f32) * o_ref[span].astype(f32), axis=0, keepdims=True)
            return scaled, row_term, tn(v_ref[0, span], scaled)

        def weigh(h, given):
            scaled, row_term, slope = given
            ds = (e_ref[0, h].astype(f32) * (slope - row_term)).astype(bf16)
            sums[0] = sums[0] + ds.astype(f32)
            return scaled, ds

        def mix(h, given):
            scaled, ds = given
            span = slice(h * HD, (h + 1) * HD)
            raw = nn(k_ref[0, span], ds)
            sums[1] = sums[1] + raw * q_ref[span].astype(f32)
            dq_ref[span] = (raw * factor).astype(bf16)
            dk_ref[0, span] = (nt(q_ref[span], ds) * LN2).astype(bf16)
            dv_ref[0, span] = nt(scaled, e_ref[0, h]).astype(bf16)

        pipeline(range(H), (0, spread), (2, weigh), (3, mix))
        acc[...] += nn(o_ref[...], da2)
        shift_sum, tau_sum = sums
        shift_out[0] = jnp.broadcast_to(jnp.sum(shift_sum, axis=1, keepdims=True), (slots, 128))
        tau_out[0] = jnp.sum(tau_sum, axis=0, keepdims=True)
        sg_ref[0:1] += nt(jnp.ones((8, rows), bf16), dq_ref[...])[:1]
        sg_ref[1:2] += nt(jnp.ones((8, slots), bf16), dv_ref[0])[:1]
        sg_ref[2:3] += jnp.sum(da2.astype(f32), axis=0, keepdims=True)

        @pl.when(item == items - 1)
        def _():
            dwo2_ref[...] = acc[...].astype(bf16)

    feature = pl.BlockSpec((D, rows), lambda i: (0, i))
    item3 = lambda a, b: pl.BlockSpec((1, a, b), lambda i: (i, 0, 0))
    return pl.pallas_call(
        kernel,
        grid=(items,),
        in_specs=[
            pl.BlockSpec((rows, D), lambda i: (i, 0)), feature, item3(D, slots), item3(D, slots),
            pl.BlockSpec((1, H, slots, rows), lambda i: (i, 0, 0, 0)), item3(H, rows), feature,
            whole((D, D)), smem(),
        ],
        out_specs=[
            feature, item3(D, slots), item3(D, slots), item3(1, rows), item3(slots, 128),
            whole((D, D)), whole((8, D)),
        ],
        out_shape=[
            sds((D, total), bf16), sds((items, D, slots), bf16), sds((items, D, slots), bf16),
            sds((items, 1, rows), f32), sds((items, slots, 128), f32), sds((D, D), bf16),
            sds((8, D), f32),
        ],
        scratch_shapes=[pltpu.VMEM((D, D), f32), pltpu.VMEM((D, rows), f32)],
        compiler_params=params(56),
        cost_estimate=cost(6 * total * D * D, 15e6),
        name="cross_backward",
    )(ds2, q, k, v, e, l, o, wo2, tau)


def between_backward(
    dq, dk, dv, ds2, n1, i1, mixed, memory, wt2, wo1, dwo2, sg_cross, sg_feed, out_plan, small,
    items, rows
):
    total = items * rows
    slots = memory.shape[1]
    n_mixed = len(mixed)
    out_pieces = piece_shapes(out_plan, 64, 4 * D, SMALL)
    m = len(out_pieces)

    def kernel(*refs):
        mixed_refs = refs[:n_mixed]
        (
            dq_ref, dk_ref, dv_ref, ds2_ref, n1_ref, i1_ref, mem_ref, wt_ref, wo1_ref,
            dwo2_ref, cross_ref, feed_ref, small_ref, ds1_ref, do1_ref, gm_ref, dwo1_ref,
        ) = refs[n_mixed : n_mixed + 17]
        give_refs = refs[n_mixed + 17 : n_mixed + 17 + m]
        acc, sg_ref, pay, extra, sem = refs[n_mixed + 17 + m :]
        item = pl.program_id(0)

        @pl.when(item == 0)
        def _():
            acc[...] = jnp.zeros_like(acc)
            sg_ref[...] = jnp.zeros_like(sg_ref)

        dy1 = tn(dq_ref[...], wt_ref[:D]) + ds2_ref[...].astype(f32)
        normal = n1_ref[...].astype(f32)
        acc[0] += nn(dq_ref[...], (normal * small_ref[3:4] + small_ref[4:5]).astype(bf16))
        ds1, dg1, dc1 = norm_backward(dy1, normal, i1_ref[...], small_ref[3:4])
        da1 = ds1.astype(bf16)
        ds1_ref[...] = da1
        sg_ref[1:2] += dg1
        sg_ref[2:3] += dc1
        sg_ref[0:1] += jnp.sum(da1.astype(f32), axis=0, keepdims=True)
        do1_ref[...] = nt(wo1_ref[...], da1).astype(bf16)
        mixed_one = jnp.concatenate([ref[...] for ref in mixed_refs], axis=0)
        acc[3] += nn(mixed_one, da1)
        mem = mem_ref[0]
        acc[1] += nn(dk_ref[0], mem)
        acc[2] += nn(dv_ref[0], mem)
        gm_ref[0] = tn(dk_ref[0], wt_ref[D : 2 * D]) + tn(dv_ref[0], wt_ref[2 * D :])

        @pl.when(item == items - 1)
        def _():
            for i in range(3):
                pay[i * D : (i + 1) * D] = acc[i].T.astype(bf16)
            pay[3 * D : 4 * D] = dwo2_ref[...]
            dwo1_ref[...] = acc[3].astype(bf16)
            extra[...] = jnp.concatenate(
                [sg_ref[:3], cross_ref[:3], feed_ref[:9], jnp.zeros((1, D), f32)]
            ).astype(bf16)
            if out_plan is None:
                pay[4 * D :] = extra[...]
            deliver(pay, give_refs, out_plan, 64, place_square, sem, extra, True)

    row_block = pl.BlockSpec((rows, D), lambda i: (i, 0))
    feature = pl.BlockSpec((D, rows), lambda i: (0, i))
    item3 = lambda a, b: pl.BlockSpec((1, a, b), lambda i: (i, 0, 0))
    outs = pl.pallas_call(
        kernel,
        grid=(items,),
        in_specs=[pl.BlockSpec((x.shape[0], rows), lambda i: (0, i)) for x in mixed]
        + [
            feature, item3(D, slots), item3(D, slots), row_block, row_block,
            pl.BlockSpec((rows, 1), lambda i: (i, 0)), item3(slots, D),
            whole((3 * D, D)), whole((D, D)), whole((D, D)), whole((8, D)), whole((16, D)), whole((24, D)),
        ],
        out_specs=[row_block, feature, item3(slots, D), whole((D, D))]
        + [any_spec()] * m,
        out_shape=[
            sds((total, D), bf16), sds((D, total), bf16), sds((items, slots, D), f32),
            sds((D, D), bf16),
        ]
        + out_pieces,
        scratch_shapes=[
            pltpu.VMEM((4, D, D), f32),
            pltpu.VMEM((8, D), f32),
            pltpu.VMEM((4 * D + (SMALL if out_plan is None else 0), D), bf16),
            pltpu.VMEM((SMALL, D), bf16),
            pltpu.SemaphoreType.DMA,
        ],
        compiler_params=params(56),
        cost_estimate=cost(8 * total * D * D, 20e6),
        name="between_backward",
    )(*mixed, dq, dk, dv, ds2, n1, i1, memory, wt2, wo1, dwo2, sg_cross, sg_feed, small)
    return outs[:4], outs[4:]


def self_backward(first, pairs, q, k, v, e, l, o, do1, tau, items, rows):
    total = items * rows
    blocks = rows // QB
    count = block_start(blocks)
    heads = 2 * pairs
    width = heads * HD

    def kernel(
        q_ref, k_ref, v_ref, e_ref, l_ref, o_ref, do_ref, tau_ref, d_ref, tau_out,
        vaug, daug, dks, dvs,
    ):
        item = pl.program_id(0)
        factor = tau_ref[item] * (1.0 / math.sqrt(HD))
        sums = [jnp.zeros((HD, QB), f32)]
        which = lax.broadcasted_iota(jnp.int32, (16, rows), 0)
        for h in range(heads):
            span = slice(h * HD, (h + 1) * HD)
            scaled = (do_ref[span].astype(f32) * l_ref[h // 2, h % 2 : h % 2 + 1]).astype(bf16)
            row_term = -jnp.sum(scaled.astype(f32) * o_ref[span].astype(f32), axis=0, keepdims=True)
            high = row_term.astype(bf16).astype(f32)
            extra = jnp.where(which == 0, high, jnp.where(which == 1, row_term - high, 0.0))
            daug[h, :HD] = scaled
            daug[h, HD:] = extra.astype(bf16)
            vaug[h, :HD] = v_ref[span]
            vaug[h, HD:] = jnp.ones((16, rows), bf16)

        def slope_of(unit, _):
            h, j = unit
            return tn(vaug[h, :, : (j + 1) * QB], daug[h, :, j * QB : (j + 1) * QB])

        def weigh(unit, slope):
            h, j = unit
            at = block_start(j)
            weight = e_ref[0, h, at : at + j + 1].reshape((j + 1) * QB, QB)
            return (weight.astype(f32) * slope).astype(bf16)

        def mix(unit, ds):
            h, j = unit
            span = slice(h * HD, (h + 1) * HD)
            here = slice(j * QB, (j + 1) * QB)
            before, upto = j * QB, (j + 1) * QB
            at = block_start(j)
            weight = e_ref[0, h, at : at + j + 1].reshape(upto, QB)
            raw = nn(k_ref[span, :upto], ds)
            queries = q_ref[span, here]
            sums[0] = sums[0] + raw * queries.astype(f32)
            d_ref[0, span, here] = (raw * factor).astype(bf16)
            dk = nt(queries, ds)
            dv = nt(daug[h, :HD, here], weight)
            if j:
                dks[h, :, :before] += dk[:, :before]
                dvs[h, :, :before] += dv[:, :before]
            dks[h, :, before:upto] = dk[:, before:]
            dvs[h, :, before:upto] = dv[:, before:]

        units = [(h, j) for j in range(blocks) for h in range(heads)]
        pipeline(units, (0, slope_of), (2, weigh), (3, mix))
        for h in range(heads):
            span = slice(h * HD, (h + 1) * HD)
            d_ref[1, span] = (dks[h] * LN2).astype(bf16)
            d_ref[2, span] = dvs[h].astype(bf16)
        tau_sum = sums[0]
        tau_out[0] = jnp.sum(tau_sum, axis=0, keepdims=True)

    feature = pl.BlockSpec((width, rows), lambda i: (first // pairs, i))
    local = pl.BlockSpec((width, rows), lambda i: (0, i))
    return pl.pallas_call(
        kernel,
        grid=(items,),
        in_specs=[
            feature, feature, feature,
            pl.BlockSpec((1, 2 * pairs, count, QB, QB), lambda i: (i, 0, 0, 0, 0)),
            pl.BlockSpec((pairs, 8, rows), lambda i: (0, 0, i)), local, feature, smem(),
        ],
        out_specs=[
            pl.BlockSpec((3, width, rows), lambda i: (0, 0, i)),
            pl.BlockSpec((1, 1, QB), lambda i: (i, 0, 0)),
        ],
        out_shape=[sds((3, width, total), bf16), sds((items, 1, QB), f32)],
        scratch_shapes=[
            pltpu.VMEM((heads, HD + 16, rows), bf16),
            pltpu.VMEM((heads, HD + 16, rows), bf16),
            pltpu.VMEM((heads, HD, rows), f32),
            pltpu.VMEM((heads, HD, rows), f32),
        ],
        compiler_params=params(56),
        cost_estimate=cost(4 * 4 * pairs * items * 2 * rows * rows * 2 * HD, 12e6),
        name="self_backward",
    )(q, k, v, in_hbm(e), l, o, do1, tau)


def self_weight_grad(x, parts, dwo1, out_plan):
    total = x.shape[0]
    n = len(parts)
    out_pieces = piece_shapes(out_plan, 64, 4 * D, SMALL)
    m = len(out_pieces)

    def kernel(*refs):
        part_refs = refs[:n]
        x_ref, dwo_ref = refs[n : n + 2]
        give_refs = refs[n + 2 : n + 2 + m]
        pay, extra, biases, sem = refs[n + 2 + m :]
        which = pl.program_id(0)
        grads = jnp.concatenate([ref[0] for ref in part_refs], axis=0)
        pay[pl.ds(pl.multiple_of(which * D, D), D)] = nn(grads, x_ref[...]).T.astype(bf16)
        biases[which] = nt(jnp.ones((8, total), bf16), grads)

        @pl.when(which == 2)
        def _():
            pay[3 * D : 4 * D] = dwo_ref[...]
            extra[...] = jnp.concatenate(
                [biases[0, :1], biases[2, :1], jnp.zeros((SMALL - 2, D), f32)]
            ).astype(bf16)
            if out_plan is None:
                pay[4 * D :] = extra[...]
            deliver(pay, give_refs, out_plan, 64, place_square, sem, extra)

    return pl.pallas_call(
        kernel,
        grid=(3,),
        in_specs=[pl.BlockSpec((1, p.shape[1], total), lambda i: (i, 0, 0)) for p in parts]
        + [whole((total, D)), whole((D, D))],
        out_specs=[any_spec()] * m,
        out_shape=out_pieces,
        scratch_shapes=[
            pltpu.VMEM((4 * D + (SMALL if out_plan is None else 0), D), bf16),
            pltpu.VMEM((SMALL, D), bf16),
            pltpu.VMEM((3, 8, D), f32),
            pltpu.SemaphoreType.DMA,
        ],
        compiler_params=params(56),
        cost_estimate=cost(6 * total * D * D, 10e6),
        name="self_weight_grad",
    )(*parts, x, dwo1)


def input_grad(ds1, parts, wt):
    n = len(parts)
    total = ds1.shape[0]

    def kernel(*refs):
        part_refs = refs[:n]
        ds1_ref, wt_ref, out_ref = refs[n:]
        grads = jnp.concatenate([ref[i] for i in range(3) for ref in part_refs], axis=0)
        out_ref[...] = ds1_ref[...].astype(f32) + tn(grads, wt_ref[...])

    return pl.pallas_call(
        kernel,
        grid=(total // ROWS,),
        in_specs=[pl.BlockSpec((3, p.shape[1], ROWS), lambda i: (0, 0, i)) for p in parts]
        + [pl.BlockSpec((ROWS, D), lambda i: (i, 0)), whole((3 * D, D))],
        out_specs=pl.BlockSpec((ROWS, D), lambda i: (i, 0)),
        out_shape=sds((total, D), f32),
        compiler_params=params(56),
        cost_estimate=cost(6 * total * D * D, 14e6),
        name="input_grad",
    )(*parts, ds1, wt)


def per_device(
    inputs,
    memory,
    tau_scale,
    delta_shift,
    horizon,
    memory_mask,
    cotangent,
    self_weights,
    cross_weights,
    feed_weights,
    small_params,
):
    items, rows = inputs.shape[0], inputs.shape[1]
    x = inputs.reshape(items * rows, D)
    direct = special()
    in_plan = GATHER_PLAN if direct else None
    out_plan = SCATTER_PLAN if direct else None
    if direct:
        is_up = lax.axis_index("wide") < 8
        width = small_params.shape[0]
        small = lax.dynamic_update_slice(
            jnp.zeros((width * 32,), bf16), small_params, (my_index() * width,)
        ).reshape(17, D)
        held = jnp.concatenate([self_weights.reshape(64, D), pad_rows(small[:2])])
        held, feed_weights, cross_weights = lax.optimization_barrier(
            (held, feed_weights, cross_weights)
        )
        held = join(gather_column(held), SMALL)
        up = feed_weights.reshape(32, 4, D).transpose(1, 0, 2).reshape(128, D)
        own_feed = jnp.where(is_up, up, feed_weights.reshape(128, D))
        held = gather_stage(held, 1, SMALL)
        top = core_hop(held, 0)
        crossed = jnp.concatenate([cross_weights.reshape(64, D), pad_rows(small[2:])])
        swapped = swap(held)
        crossed = join(gather_column(after(crossed, swapped)), SMALL)
        self_pieces = [held, top, swapped, swap(after(top, crossed))]
        crossed, own_feed, _ = lax.optimization_barrier((crossed, own_feed, self_pieces[3]))
        cross_came = core_hop(crossed, 1)
        fed_came = column_step(own_feed, 0)
    else:
        small = lax.all_gather(small_params, W, axis=0, tiled=True).reshape(17, D)
        full = lax.all_gather(self_weights, W, axis=0, tiled=True).reshape(4 * D, D)
        self_pieces = [jnp.concatenate([full, pad_rows(small[:2])])]
        full = lax.all_gather(cross_weights, W, axis=0, tiled=True).reshape(4 * D, D)
        cross_pieces = [jnp.concatenate([full, pad_rows(small[2:])])]
        full = lax.all_gather(feed_weights, W, axis=0, tiled=True)
        up = full[: D * FF].reshape(16, 32, 4, D).transpose(0, 2, 1, 3).reshape(4 * D, D)
        feed_pieces = [jnp.concatenate([up, full[D * FF :].reshape(4 * D, D)])]

    q1, k1, v1, wt1, wo1 = project_self(x, self_pieces, in_plan, tau_scale)
    if direct:
        cross_came, fed_came, q1 = lax.optimization_barrier((cross_came, fed_came, q1))
        crossed = join([crossed, cross_came], SMALL)
        cross_came = core_hop(crossed, 0)
        fed = join([own_feed, fed_came])
        fed_came = column_step(fed, 1)
        q1 = after(q1, crossed, fed)
    first = 0
    kept = []
    for pairs in GROUPS:
        if kept:
            q1 = after(q1, kept[-1][3])
            if direct:
                fed_came, cross_came, o1 = lax.optimization_barrier((fed_came, cross_came, kept[-1][3]))
                kept[-1] = kept[-1][:3] + (o1,) + kept[-1][4:]
                fed = join([fed, fed_came])
                feed_came = core_hop(fed, 1)
                cross_pieces = [crossed, cross_came, swap(crossed), swap(cross_came)]
                q1 = after(q1, fed, cross_came)
        kept.append((first, pairs) + tuple(attend_self(first, pairs, q1, k1, v1, items, rows)))
        first += pairs
    if direct:
        feed_came, wo1, *swapped = lax.optimization_barrier(
            (feed_came, wo1, *cross_pieces[2:], kept[-1][3])
        )
        cross_pieces[2:] = swapped[:2]
        fed = join([fed, feed_came])
        feed_came = core_hop(fed, 0)
        feed_pieces = [fed, feed_came, swap(fed)]
        wo1 = after(wo1, fed)
    mixed = [group[3] for group in kept]
    n1, i1, n2, i2, q2, k2, v2, e2, l2, o2, wt2, wo2, small = cross_forward(
        x, mixed, wo1, cross_pieces, in_plan, tau_scale, memory, delta_shift, memory_mask
    )
    if direct:
        feed_pieces.append(swap(after(feed_came, n2)))
    output, ds2, sg_feed, feed_give = feed(
        n2, i2, feed_pieces, in_plan, out_plan, small, horizon,
        cotangent.reshape(items * rows, D), rows,
    )
    if direct:
        feed_steps = Scatter(*feed_give, 128)
    dq2, dk2, dv2, tau_two, shift_sum, dwo2, sg_cross = cross_backward(
        ds2, q2, k2, v2, e2, l2, o2, wo2, tau_scale, items, rows
    )
    if direct:
        feed_steps.wait(dq2)
        dq2 = after(dq2, feed_steps.first())
    (ds1, do1, grad_memory, dwo1), cross_give = between_backward(
        dq2, dk2, dv2, ds2, n1, i1, mixed, memory, wt2, wo1, dwo2, sg_cross, sg_feed, out_plan,
        small, items, rows,
    )
    if direct:
        cross_steps = Scatter(*cross_give, 64, SMALL)
        feed_steps.wait(do1)
        do1 = after(do1, feed_steps.second())
    parts, taus = [], []
    for first, pairs, e1, o1, l1 in kept:
        if len(parts) == 1:
            do1 = after(do1, parts[0])
            if direct:
                feed_steps.wait(parts[0])
                cross_steps.wait(parts[0])
                do1 = after(do1, feed_steps.column(), cross_steps.first())
        part, tau_one = self_backward(
            first, pairs, q1, k1, v1, e1, l1, o1, do1, tau_scale, items, rows
        )
        parts.append(part)
        taus.append(tau_one)
    if direct:
        cross_steps.wait(parts[-1])
        dwo1 = after(dwo1, cross_steps.second(), *feed_steps.came[1:])
    self_give = self_weight_grad(x, parts, dwo1, out_plan)
    if direct:
        keep, send = self_give
        self_steps = Scatter(keep, after(send, cross_steps.came), 64, SMALL)
        feed_steps.wait_column(keep)
        tau_two, shift_sum, taus, _ = lax.optimization_barrier((tau_two, shift_sum, taus, keep))
    grad_tau = sum(jnp.sum(t, axis=(1, 2)) for t in [tau_two] + taus) / (LOG2E * tau_scale)
    grad_delta = shift_sum[:, :, 0]
    if direct:
        (own_feed,) = feed_steps.total()
        up = own_feed.reshape(4, 32, D).transpose(1, 0, 2).reshape(-1)
        grad_feed = jnp.where(is_up, up, own_feed.reshape(-1))
        self_steps.wait(grad_feed, grad_tau, grad_delta)
        sent = self_steps.first()
        cross_steps.wait(sent)
        ds1 = after(ds1, sent, cross_steps.column_one())
    grad_inputs = input_grad(ds1, parts, wt1)
    if direct:
        self_steps.wait(grad_inputs, cross_steps.came)
        sent = self_steps.second()
        cross_steps.wait(sent)
        cross_steps.column_two()
        cross_steps.wait(self_steps.column())

    if direct:
        grad_cross, small_rest = cross_steps.total_two()
        grad_self, small_grad = self_steps.total()
        grad_self = grad_self.reshape(-1)
        grad_cross = grad_cross.reshape(-1)
        small_grad = jnp.concatenate([small_grad[:2], small_rest[:15]]).reshape(-1)
        grad_small = lax.dynamic_slice(small_grad, (my_index() * width,), (width,))
    else:
        scatter = lambda v: lax.psum_scatter(v.reshape(-1), W, scatter_dimension=0, tiled=True)
        full, rest = self_give[0].astype(f32), cross_give[0].astype(f32)
        grad_self, grad_cross = scatter(full[: 4 * D]), scatter(rest[: 4 * D])
        small_grad = jnp.concatenate([full[4 * D : 4 * D + 2], rest[4 * D : 4 * D + 15]])
        grad_small = scatter(small_grad)
        full = feed_give[0].astype(f32)
        up = full[: 4 * D].reshape(16, 4, 32, D).transpose(0, 2, 1, 3).reshape(-1)
        grad_feed = scatter(jnp.concatenate([up, full[4 * D :].reshape(-1)]))
    return (
        output.reshape(items, rows, D),
        grad_inputs.reshape(items, rows, D),
        grad_memory,
        grad_tau,
        grad_delta,
        grad_self,
        grad_cross,
        grad_feed,
        grad_small,
    )


def solution(mesh):
    whole_mesh = P(W)
    rows3 = P(W, None, None)
    rows2 = P(W, None)
    return jax.shard_map(
        per_device,
        mesh=mesh,
        in_specs=(
            rows3, rows3, whole_mesh, rows2, whole_mesh, rows2, rows3,
            whole_mesh, whole_mesh, whole_mesh, whole_mesh,
        ),
        out_specs=(
            rows3, rows3, rows3, whole_mesh, rows2, whole_mesh, whole_mesh, whole_mesh, whole_mesh,
        ),
        check_vma=False,
    )
```
